256 devices in a mesh: section: 4 (over x_lo, core), band: 64 (over y, x_hi, z).
Axes of the slice: x: 4 (x_hi: 2, x_lo: 2; x = x_hi * 2 + x_lo), y: 4, z: 8, core: 2. Of those that a mesh axis runs over, the one named last changes fastest.
Arguments:
- fields: bfloat16 [4, 69, 512, 1024], P(None, None, 'band', 'section'), may hold values from -6 to 6
- conv_weight: bfloat16 [9, 69, 256], replicated, may hold values from -0.25 to 0.25
- kernel_blocks: bfloat16 [64, 128, 128], P('band'), may hold values from -0.25 to 0.25
- block_coords: int32 [64, 2], P('band'), may hold values from 0 to 31, as said below
- forcing_table: bfloat16 [24, 4096], replicated, may hold values from -6 to 6
- forcing_codes: int32 [2, 4, 256, 32], P(None, None, 'band', 'section'), may hold values from 0 to 23
- cotangent: bfloat16 [4, 256, 32, 4096], P(None, 'band', 'section'), may hold values from -0.078125 to 0.078125
Outputs:
- latent_next: bfloat16 [4, 256, 32, 4096], P(None, 'band', 'section')
- grad_conv: float32 [9, 69, 256], replicated
- grad_blocks: float32 [64, 128, 128], P('band')
- grad_forcing: float32 [24, 4096], replicated
The draws below stay inside these ranges and needn't reach their ends.
Inputs may be any that keep to these rules, and one draw needn't show every extreme that they name: The rows of block_coords name distinct blocks of the 32 x 32 block grid.
All inputs are finite; a program needn't handle non-finite values.
Results may differ from the reference program's by a relative error of at most 0.0054.
Values may be sent and summed in bfloat16 or wider, within the bound.
No kernel may reach another device: no remote copies, remote signals or barrier semaphores. Data moves between devices by JAX's collectives and lax.ppermute only.
A program may use at most 128 MiB of HBM per device.

```python
import jax
import jax.numpy as jnp
from jax import lax

C = 69
CH = 256
GROUP = 16
BLK = 128
NF = 24
STEPS = 2
SAMPLES = 4
KW = 4096
NB = 32
NNZ = 64
NLAT = 512
NLON = 1024
NLR = 256
NG_ALL = 32
TOKENS = 32768


def draw_block_coords(key, part):
    key = jax.random.fold_in(key, 7)
    chosen = jax.random.permutation(key, NB * NB)[:NNZ]
    return jnp.stack([chosen // NB, chosen % NB], axis=1).astype(jnp.int32)


def set_ends(result, own_key, low, top_value):
    spot = [jax.random.randint(jax.random.fold_in(own_key, axis), (), 0, length) for axis, length in enumerate(result.shape)]
    longest = result.shape.index(max(result.shape))
    beside = spot[:longest] + [(spot[longest] + 1) % result.shape[longest]] + spot[longest + 1:]
    return result.at[tuple(spot)].set(low).at[tuple(beside)].set(top_value)


def shard_levels(key, extent, cuts, low, largest):
    def one(dim, blocks):
        heights = jax.random.uniform(jax.random.fold_in(jax.random.fold_in(key, 6), dim), (blocks,), jnp.float32, low / len(cuts), largest / len(cuts))
        return jnp.repeat(jnp.exp(heights), extent[dim] // blocks).reshape((-1,) + (1,) * (len(extent) - dim - 1))

    factor_of = one(*cuts[0])
    for cut in cuts[1:]:
        factor_of = factor_of * one(*cut)
    return factor_of


def noise(rng, shape, scale, limit, cuts=(), kind=jnp.bfloat16):
    entries = scale * jax.random.normal(rng, shape, jnp.float32)
    if cuts:
        entries = entries * shard_levels(rng, shape, cuts, -0.22, 0.18)
    return jnp.clip(entries, -limit, limit).astype(kind)


def setup_inputs(seed: int = 0) -> dict:
    streams_of = jax.random.split(jax.random.key(seed), 8)
    return {
        "fields": noise(streams_of[0], (SAMPLES, C, NLAT, NLON), 1.0, 6.0, ((2, 64), (3, 4))),
        "conv_weight": noise(streams_of[1], (9, C, CH), (9 * C) ** -0.5, 0.25),
        "kernel_blocks": noise(streams_of[2], (NNZ, BLK, BLK), (4 * BLK) ** -0.5, 0.25, ((0, 64),)),
        "block_coords": draw_block_coords(jax.random.fold_in(streams_of[7], 71), 0),
        "forcing_table": noise(streams_of[4], (NF, KW), 0.5, 6.0),
        "forcing_codes": set_ends(jax.random.randint(streams_of[5], (STEPS, SAMPLES, NLR, NG_ALL), 0, NF), jax.random.fold_in(streams_of[5], 1), 0, NF - 1).astype(jnp.int32),
        "cotangent": noise(streams_of[6], (SAMPLES, NLR, NG_ALL, KW), (TOKENS ** -0.5), 0.078125, ((1, 64), (2, 4))),
    }


def extend(fields):
    north = jnp.zeros_like(fields[:, :, :1, :])
    padded = jnp.concatenate([north, fields], axis=2)
    return jnp.concatenate([padded[:, :, :, -1:], padded], axis=3)

def window_of(padded_one, row_tap, col_tap, half_rows, half_cols):
    return lax.slice(padded_one, (0, row_tap, col_tap), (padded_one.shape[0], row_tap + 2 * half_rows - 1, col_tap + 2 * half_cols - 1), (1, 2, 2))

def encode_one(padded_one, conv_weight):
    half_rows = (padded_one.shape[1] - 1) // 2
    half_cols = (padded_one.shape[2] - 1) // 2
    weights = conv_weight.astype(jnp.float32)
    summed = jnp.zeros((weights.shape[2], half_rows, half_cols), jnp.float32)
    for row_tap in range(3):
        for col_tap in range(3):
            window = window_of(padded_one, row_tap, col_tap, half_rows, half_cols).astype(jnp.float32)
            summed = summed + jnp.einsum('io,irc->orc', weights[3 * row_tap + col_tap], window)
    return summed

def to_tokens(latent):
    samples, channels, lat_rows, lat_cols = latent.shape
    shaped = latent.reshape(samples, channels, lat_rows, lat_cols // GROUP, GROUP)
    return jnp.transpose(shaped, (0, 2, 3, 1, 4)).reshape(samples, lat_rows, lat_cols // GROUP, channels * GROUP)

def from_tokens(tokens):
    samples, lat_rows, groups, width = tokens.shape
    shaped = tokens.reshape(samples, lat_rows, groups, width // GROUP, GROUP)
    return jnp.transpose(shaped, (0, 3, 1, 2, 4)).reshape(samples, width // GROUP, lat_rows, groups * GROUP)

def apply_blocks(vectors, blocks, coords, transposed):

    def one_block(index, summed):
        source = coords[index, 0] * BLK
        target = coords[index, 1] * BLK
        if transposed:
            source, target = (target, source)
        part = lax.dynamic_slice_in_dim(vectors, source, BLK, 1)
        if transposed:
            product = lax.dot_general(part, blocks[index], (((1,), (1,)), ((), ())), preferred_element_type=jnp.float32)
        else:
            product = jnp.dot(part, blocks[index], preferred_element_type=jnp.float32)
        current = lax.dynamic_slice_in_dim(summed, target, BLK, 1)
        return lax.dynamic_update_slice_in_dim(summed, current + product, target, 1)
    return lax.fori_loop(0, blocks.shape[0], one_block, jnp.zeros(vectors.shape, jnp.float32))

def reference(fields, conv_weight, kernel_blocks, block_coords, forcing_table, forcing_codes, cotangent):
    padded = extend(fields)
    latent = lax.map(lambda padded_one: encode_one(padded_one, conv_weight), padded)
    state_zero = to_tokens(latent).reshape(-1, KW).astype(jnp.bfloat16)
    codes = forcing_codes.reshape(STEPS, -1)
    states = [state_zero]
    for step_index in range(STEPS):
        current = states[-1]
        pushed = apply_blocks(current, kernel_blocks, block_coords, False)
        forcing = forcing_table[codes[step_index]].astype(jnp.float32)
        states.append((current.astype(jnp.float32) + pushed + forcing).astype(jnp.bfloat16))
    latent_next = states[-1].reshape(SAMPLES, NLR, NG_ALL, KW)
    adjoints = [cotangent.reshape(-1, KW)]
    for step_index in range(STEPS):
        later = adjoints[0]
        pulled = apply_blocks(later, kernel_blocks, block_coords, True)
        adjoints.insert(0, (later.astype(jnp.float32) + pulled).astype(jnp.bfloat16))
    grad_forcing = jnp.zeros((NF, KW), jnp.float32)
    for step_index in range(STEPS):
        grad_forcing = grad_forcing + jax.ops.segment_sum(adjoints[step_index + 1].astype(jnp.float32), codes[step_index], NF)
    stack_states = jnp.concatenate(states[:STEPS], axis=0)
    stack_adjoint = jnp.concatenate(adjoints[1:], axis=0)

    def block_grad(index):
        left = lax.dynamic_slice_in_dim(stack_states, block_coords[index, 0] * BLK, BLK, 1)
        right = lax.dynamic_slice_in_dim(stack_adjoint, block_coords[index, 1] * BLK, BLK, 1)
        return lax.dot_general(left, right, (((0,), (0,)), ((), ())), preferred_element_type=jnp.float32)
    grad_blocks = lax.map(block_grad, jnp.arange(NNZ, dtype=jnp.int32))
    latent_adjoint = from_tokens(adjoints[0].reshape(SAMPLES, NLR, NG_ALL, KW))

    def conv_grad(summed, pair):
        padded_one, adjoint_one = pair
        half_rows = adjoint_one.shape[1]
        half_cols = adjoint_one.shape[2]
        adjoint_wide = adjoint_one.astype(jnp.float32)
        pieces_list = []
        for row_tap in range(3):
            for col_tap in range(3):
                window = window_of(padded_one, row_tap, col_tap, half_rows, half_cols).astype(jnp.float32)
                pieces_list.append(jnp.einsum('irc,orc->io', window, adjoint_wide))
        return (summed + jnp.stack(pieces_list), None)
    grad_conv, unused = lax.scan(conv_grad, jnp.zeros((9, C, CH), jnp.float32), (padded, latent_adjoint))
    return (latent_next, grad_conv, grad_blocks, grad_forcing)
```

```python
import functools

import jax
import jax.numpy as jnp
from jax import lax
from jax.experimental import pallas as pl
from jax.experimental.pallas import tpu as pltpu
from jax.sharding import Mesh, PartitionSpec as P

BAND = ("y", "xh", "z")
SECTION = ("xl", "core")
ALL = ("xl", "core", "y", "xh", "z")
CIN, COUT, ROWS, PAD = 69, 256, 16, 80
TOK, WIDTH, NBLK, NNZ, NCODE = 128, 4096, 32, 64, 24
F32, BF16 = jnp.float32, jnp.bfloat16
VMEM_LIMIT = 56 * 1024 * 1024


def dot(a, b):
    return jnp.dot(a, b, preferred_element_type=F32)


def patches_kernel(fields_ref, north_ref, z_ref, east_ref, y0, y1, n0, n1):
    row = lax.broadcasted_iota(jnp.int32, (256, 256), 0)
    col = lax.broadcasted_iota(jnp.int32, (256, 256), 1)
    order = (row == (col & 7) * 32 + (col >> 3)).astype(BF16)

    def spread(step, carry):
        rows = pl.ds(pl.multiple_of(step * 368, 16), 368)
        mixed = dot(fields_ref[rows, :], order)
        y0[rows, :] = mixed[:, :128]
        y1[rows, :] = mixed[:, 128:]
        return carry

    lax.fori_loop(0, 6, spread, 0)
    y0[2208:2304, :] = jnp.zeros((96, 128), F32)
    y1[2208:2304, :] = jnp.zeros((96, 128), F32)
    mixed = dot(north_ref[...], order)
    n0[...] = mixed[:, :128]
    n1[...] = mixed[:, 128:]
    lane = lax.broadcasted_iota(jnp.int32, (16, 128), 1)

    def chunk(step, carry):
        for half, (rows_ref, top_ref) in enumerate(((y0, n0), (y1, n1))):
            for a in range(3):
                parts = []
                for s in range(4):
                    for r in range(4):
                        lat = 2 * r + a - 1
                        if lat < 0:
                            at = pl.ds(pl.multiple_of(s * PAD + step * 16, 16), 16)
                            parts.append(top_ref[at, :])
                        else:
                            at = pl.ds(s * CIN * 8 + lat + step * 128, 16, stride=8)
                            parts.append(rows_ref[at, :])
                for bit in (1, 2, 4, 8):
                    high = (lane & (8 * bit)) != 0
                    for i in range(16):
                        if i & bit:
                            continue
                        low_part, high_part = parts[i], parts[i | bit]
                        parts[i] = jnp.where(high, pltpu.roll(high_part, 8 * bit, 1), low_part)
                        parts[i | bit] = jnp.where(
                            high, high_part, pltpu.roll(low_part, 128 - 8 * bit, 1)
                        )
                for q in range(16):
                    at = pl.multiple_of((half * 16 + q + 1) * PAD + step * 16, 16)
                    z_ref[a, pl.ds(at, 16), :] = parts[q].astype(BF16)
                if half == 1:
                    at = pl.multiple_of(a * PAD + step * 16, 16)
                    east_ref[pl.ds(at, 16), :] = parts[15].astype(BF16)
        return carry

    lax.fori_loop(0, PAD // 16, chunk, 0)
    for a in range(3):
        z_ref[a, 0:PAD, :] = jnp.zeros((PAD, 128), BF16)


def make_patches(fields, north):
    return pl.pallas_call(
        patches_kernel,
        out_shape=(
            jax.ShapeDtypeStruct((3, 33 * PAD, 128), BF16),
            jax.ShapeDtypeStruct((3 * PAD, 128), BF16),
        ),
        in_specs=[pl.BlockSpec(memory_space=pltpu.VMEM)] * 2,
        out_specs=(pl.BlockSpec(memory_space=pltpu.VMEM),) * 2,
        scratch_shapes=[
            pltpu.VMEM((2304, 128), F32),
            pltpu.VMEM((2304, 128), F32),
            pltpu.VMEM((320, 128), F32),
            pltpu.VMEM((320, 128), F32),
        ],
        compiler_params=pltpu.CompilerParams(vmem_limit_bytes=VMEM_LIMIT),
        cost_estimate=pl.CostEstimate(flops=2 * 2528 * 256 * 256, bytes_accessed=4000000, transcendentals=0),
    )(fields, north)


def place(m):
    return (m // 64) % 2, m // 128, m % 64


def main_kernel(
    coords_ref, z_ref, west_ref, weight_ref, blocks_ref, table_ref, codes_ref, cot_ref,
    next_ref, out_ref,
    p0, wt, wf, sa, sb, aa, ab, at0, gc, left,
):
    lane = lax.broadcasted_iota(jnp.int32, (PAD, 128), 1)
    for a in range(3):
        own = pltpu.roll(z_ref[a, 32 * PAD:33 * PAD, :].astype(F32), 1, 1)
        other = pltpu.roll(west_ref[a * PAD:(a + 1) * PAD, :].astype(F32), 128 - 7, 1)
        p0[a, 0:PAD, :] = jnp.where((lane & 7) == 0, other, own).astype(BF16)
        p0[a, PAD:3 * PAD, :] = z_ref[a, PAD:3 * PAD, :]
        wf[...] = jnp.zeros(wf.shape, F32)
        for b in range(3):
            wf[b * PAD:b * PAD + CIN, :] = weight_ref[3 * a + b].astype(F32)
        wt[a] = wf[...].T.astype(BF16)

    def encode(patches, k):
        total = dot(wt[0], patches(0)) + dot(wt[1], patches(1)) + dot(wt[2], patches(2))
        sa[pl.ds(k, COUT, stride=16), :] = total

    def patch_of(k):
        rows = pl.ds(pl.multiple_of(k * 2 * PAD, 16), 3 * PAD)
        return lambda a: z_ref[a, rows, :]

    encode(lambda a: p0[a], 0)

    def encode_step(k, carry):
        encode(patch_of(k), k)
        return carry

    lax.fori_loop(1, 16, encode_step, 0)

    code = lax.broadcasted_iota(jnp.int32, (NCODE, TOK), 0)
    hot0 = (code == codes_ref[0:1, :]).astype(BF16)
    hot1 = (code == codes_ref[1:2, :]).astype(BF16)
    over_rows = (((0,), (0,)), ((), ()))

    def begin(b, carry):
        rows = pl.ds(pl.multiple_of(b * 128, 128), 128)
        state = sa[rows, :].astype(BF16)
        sb[rows, 0:128] = state
        forcing = lax.dot_general(table_ref[:, rows], hot0, over_rows, preferred_element_type=F32)
        sa[rows, :] = state.astype(F32) + forcing
        cot = cot_ref[:, rows]
        ab[b, 128:256, :] = cot
        aa[b] = cot.astype(F32)
        return carry

    lax.fori_loop(0, NBLK, begin, 0)

    def step_of(adjoint_rows, state_lanes):
        def body(group, carry):
            items = []
            for u in range(8):
                n = group * 8 + u
                i, j = coords_ref[n, 0], coords_ref[n, 1]
                block = blocks_ref[n, 0:128, :]
                pulled = dot(ab[j, adjoint_rows, :], block)
                source = pl.ds(pl.multiple_of(i * 128, 128), 128)
                pushed = dot(block, sb[source, state_lanes])
                items.append((i, j, pulled, pushed))
            for i, j, pulled, pushed in items:
                target = pl.ds(pl.multiple_of(j * 128, 128), 128)
                aa[i] = aa[i] + pulled
                sa[target, :] = sa[target, :] + pushed
            return carry

        lax.fori_loop(0, NNZ // 8, body, 0)

    step_of(slice(128, 256), slice(0, 128))

    def between(b, carry):
        rows = pl.ds(pl.multiple_of(b * 128, 128), 128)
        state = sa[rows, :].astype(BF16)
        sb[rows, 128:256] = state
        forcing = lax.dot_general(table_ref[:, rows], hot1, over_rows, preferred_element_type=F32)
        sa[rows, :] = state.astype(F32) + forcing
        adjoint = aa[b].astype(BF16)
        ab[b, 0:128, :] = adjoint
        aa[b] = adjoint.astype(F32)
        return carry

    lax.fori_loop(0, NBLK, between, 0)
    step_of(slice(0, 128), slice(128, 256))

    def end(b, carry):
        rows = pl.ds(pl.multiple_of(b * 128, 128), 128)
        next_ref[:, rows] = sa[rows, :].T.astype(BF16)
        at0[rows, :] = aa[b].T
        return carry

    lax.fori_loop(0, NBLK, end, 0)

    def block_grads(group, carry):
        for u in range(4):
            n = group * 4 + u
            i, j = coords_ref[n, 0], coords_ref[n, 1]
            grad = dot(sb[pl.ds(pl.multiple_of(i * 128, 128), 128), :], ab[j])
            for c in range(2):
                for x in range(2):
                    out_ref[c, x, n, 0:32, :] = grad[(2 * c + x) * 32:(2 * c + x + 1) * 32, :]
        return carry

    lax.fori_loop(0, NNZ // 4, block_grads, 0)

    hot = jnp.concatenate([hot0, hot1], axis=1)
    for j in range(NBLK):
        term = dot(hot, ab[j])
        for third in range(3):
            c, x, n = place(3 * j + third)
            out_ref[c, x, n, 32:40, :] = term[third * 8:(third + 1) * 8, :]

    def conv_grads(patches, k, first):
        adjoint = at0[pl.ds(k, COUT, stride=16), :].astype(BF16)
        for a in range(3):
            term = lax.dot_general(
                patches(a), adjoint, (((1,), (1,)), ((), ())), preferred_element_type=F32
            )
            gc[a] = term if first else gc[a] + term

    conv_grads(lambda a: p0[a], 0, True)

    def conv_grads_step(k, carry):
        conv_grads(patch_of(k), k, False)
        return carry

    lax.fori_loop(1, 16, conv_grads_step, 0)
    left[...] = jnp.zeros(left.shape, F32)
    for tap in range(9):
        a, b = divmod(tap, 3)
        for half in range(2):
            lanes = slice(half * 128, (half + 1) * 128)
            for g in range(8):
                c, x, n = place(96 + (tap * 8 + g) * 2 + half)
                out_ref[c, x, n, 32:40, :] = gc[a, b * PAD + g * 8:b * PAD + g * 8 + 8, lanes]
            at = 5 * (2 * tap + half)
            left[at:at + 5, :] = gc[a, b * PAD + 64:b * PAD + CIN, lanes]
    for m in range(240, 256):
        c, x, n = place(m)
        at = (m - 240) * 8
        out_ref[c, x, n, 32:40, :] = left[at:at + 8, :]


def run_main(coords, z, west, weight, blocks, table, codes, cot):
    vmem = pl.BlockSpec(memory_space=pltpu.VMEM)
    return pl.pallas_call(
        main_kernel,
        out_shape=(
            jax.ShapeDtypeStruct((TOK, WIDTH), BF16),
            jax.ShapeDtypeStruct((2, 2, 64, 40, 128), F32),
        ),
        in_specs=[pl.BlockSpec(memory_space=pltpu.SMEM)] + [vmem] * 7,
        out_specs=(vmem, vmem),
        scratch_shapes=[
            pltpu.VMEM((3, 3 * PAD, 128), BF16),
            pltpu.VMEM((3, COUT, 3 * PAD), BF16),
            pltpu.VMEM((3 * PAD, COUT), F32),
            pltpu.VMEM((WIDTH, TOK), F32),
            pltpu.VMEM((WIDTH, 2 * TOK), BF16),
            pltpu.VMEM((NBLK, TOK, 128), F32),
            pltpu.VMEM((NBLK, 2 * TOK, 128), BF16),
            pltpu.VMEM((WIDTH, TOK), F32),
            pltpu.VMEM((3, 3 * PAD, COUT), F32),
            pltpu.VMEM((128, 128), F32),
        ],
        compiler_params=pltpu.CompilerParams(vmem_limit_bytes=VMEM_LIMIT),
        cost_estimate=pl.CostEstimate(flops=3 * 10**9, bytes_accessed=14 * 10**6, transcendentals=0),
    )(coords, z, west, weight, blocks, table, codes, cot)


def unpack_kernel(sums_ref, conv_ref, forcing_ref, left):
    for j in range(NBLK):
        for third in range(3):
            forcing_ref[third * 8:(third + 1) * 8, j * 128:(j + 1) * 128] = sums_ref[3 * j + third]
    for m in range(12):
        left[m * 8:(m + 1) * 8, :] = sums_ref[240 + m]
    for tap in range(9):
        for half in range(2):
            lanes = slice(half * 128, (half + 1) * 128)
            for g in range(8):
                conv_ref[tap, g * 8:(g + 1) * 8, lanes] = sums_ref[96 + (tap * 8 + g) * 2 + half]
            at = 5 * (2 * tap + half)
            conv_ref[tap, 64:CIN, lanes] = left[at:at + 5, :]


def unpack(sums):
    vmem = pl.BlockSpec(memory_space=pltpu.VMEM)
    return pl.pallas_call(
        unpack_kernel,
        out_shape=(
            jax.ShapeDtypeStruct((9, CIN, COUT), F32),
            jax.ShapeDtypeStruct((NCODE, WIDTH), F32),
        ),
        in_specs=[vmem],
        out_specs=(vmem, vmem),
        scratch_shapes=[pltpu.VMEM((96, 128), F32)],
        compiler_params=pltpu.CompilerParams(vmem_limit_bytes=VMEM_LIMIT),
    )(sums)


def swap(value, axes, pairs):
    return lax.ppermute(value, axes, pairs)


def per_device(
    fields, conv_weight, kernel_blocks, block_coords, forcing_table, forcing_codes, cotangent
):
    top = jnp.pad(fields[:, :, 7, :], ((0, 0), (0, PAD - CIN), (0, 0))).reshape(4 * PAD, 256)
    north = lax.ppermute(top, BAND, [(i, i + 1) for i in range(63)])

    marks = jnp.pad(block_coords.astype(BF16), ((0, 15), (0, 126)))
    payload = jnp.concatenate([kernel_blocks[0].T, marks], axis=0)
    spread = jnp.broadcast_to(payload[None], (NNZ,) + payload.shape)
    z, east = make_patches(fields.reshape(-1, 256), north)
    west = lax.ppermute(east, SECTION, [(i, (i + 1) % 4) for i in range(4)])
    gathered = lax.all_to_all(spread, BAND, 0, 0, tiled=True)
    coords = gathered[:, 128, 0:2].astype(jnp.int32)

    latent_next, partial = run_main(
        coords, z, west, conv_weight, gathered, forcing_table,
        forcing_codes.reshape(2, TOK), cotangent.reshape(TOK, WIDTH),
    )
    chip = lax.psum_scatter(partial, "core", scatter_dimension=0, tiled=True)
    parts = lax.all_to_all(
        chip.reshape(128, 40, 128).astype(BF16), ("xl",) + BAND, 0, 0, tiled=True
    )
    sums = jnp.sum(parts.astype(F32), axis=0)
    own = sums[0:32]
    shared = jnp.broadcast_to(sums[None, 32:40].astype(BF16), (256, 8, 128))
    others = [
        lax.ppermute(own, SECTION, [(i, i ^ flip) for i in range(4)]) for flip in (1, 2, 3)
    ]
    everyone = lax.all_to_all(shared, ALL, 0, 0, tiled=True)
    grad_conv, grad_forcing = unpack(everyone.astype(F32))
    section = 2 * lax.axis_index("xl") + lax.axis_index("core")
    quarters = jnp.stack([own] + others)
    order = jnp.stack([section ^ (2 * (q % 2) + q // 2) for q in range(4)])
    grad_blocks = jnp.take(quarters, order, axis=0).reshape(1, 128, 128)
    return (latent_next.reshape(cotangent.shape), grad_conv, grad_blocks, grad_forcing)


def solution(mesh):
    fine = Mesh(mesh.devices.reshape(2, 2, 4, 2, 8), ALL)
    return jax.shard_map(
        per_device,
        mesh=fine,
        in_specs=(
            P(None, None, BAND, SECTION),
            P(),
            P(BAND, None, None),
            P(BAND, None),
            P(),
            P(None, None, BAND, SECTION),
            P(None, BAND, SECTION, None),
        ),
        out_specs=(P(None, BAND, SECTION, None), P(), P(BAND, None, None), P()),
        check_vma=False,
    )
```

```python
import jax
import jax.numpy as jnp
from jax import lax
from jax.experimental import pallas as pl
from jax.experimental.pallas import tpu as pltpu
from jax.sharding import Mesh, PartitionSpec as P

BAND = ("y", "xh", "z")
SECTION = ("xl", "core")
ALL = ("xl", "core", "y", "xh", "z")
CIN, COUT, ROWS, PAD = 69, 256, 16, 80
TOK, WIDTH, NBLK, NNZ, NCODE = 128, 4096, 32, 64, 24
F32, BF16 = jnp.float32, jnp.bfloat16
VMEM_LIMIT = 56 * 1024 * 1024


def dot(a, b):
    return jnp.dot(a, b, preferred_element_type=F32)


def patches_kernel(fields_ref, north_ref, z_ref, east_ref, y0, y1, n0, n1):
    row = lax.broadcasted_iota(jnp.int32, (256, 256), 0)
    col = lax.broadcasted_iota(jnp.int32, (256, 256), 1)
    order = (row == (col & 7) * 32 + (col >> 3)).astype(BF16)

    def spread(step, carry):
        rows = pl.ds(pl.multiple_of(step * 368, 16), 368)
        mixed = dot(fields_ref[rows, :], order)
        y0[rows, :] = mixed[:, :128]
        y1[rows, :] = mixed[:, 128:]
        return carry

    lax.fori_loop(0, 6, spread, 0)
    y0[2208:2304, :] = jnp.zeros((96, 128), F32)
    y1[2208:2304, :] = jnp.zeros((96, 128), F32)
    mixed = dot(north_ref[...], order)
    n0[...] = mixed[:, :128]
    n1[...] = mixed[:, 128:]
    lane = lax.broadcasted_iota(jnp.int32, (16, 128), 1)

    def chunk(step, carry):
        for half, (rows_ref, top_ref) in enumerate(((y0, n0), (y1, n1))):
            for a in range(3):
                parts = []
                for s in range(4):
                    for r in range(4):
                        lat = 2 * r + a - 1
                        if lat < 0:
                            at = pl.ds(pl.multiple_of(s * PAD + step * 16, 16), 16)
                            parts.append(top_ref[at, :])
                        else:
                            at = pl.ds(s * CIN * 8 + lat + step * 128, 16, stride=8)
                            parts.append(rows_ref[at, :])
                for bit in (1, 2, 4, 8):
                    high = (lane & (8 * bit)) != 0
                    for i in range(16):
                        if i & bit:
                            continue
                        low_part, high_part = parts[i], parts[i | bit]
                        parts[i] = jnp.where(high, pltpu.roll(high_part, 8 * bit, 1), low_part)
                        parts[i | bit] = jnp.where(
                            high, high_part, pltpu.roll(low_part, 128 - 8 * bit, 1)
                        )
                for q in range(16):
                    at = pl.multiple_of((half * 16 + q + 1) * PAD + step * 16, 16)
                    z_ref[a, pl.ds(at, 16), :] = parts[q].astype(BF16)
                if half == 1:
                    at = pl.multiple_of(a * PAD + step * 16, 16)
                    east_ref[pl.ds(at, 16), :] = parts[15].astype(BF16)
        return carry

    lax.fori_loop(0, PAD // 16, chunk, 0)
    for a in range(3):
        z_ref[a, 0:PAD, :] = jnp.zeros((PAD, 128), BF16)


def make_patches(fields, north):
    return pl.pallas_call(
        patches_kernel,
        out_shape=(
            jax.ShapeDtypeStruct((3, 33 * PAD, 128), BF16),
            jax.ShapeDtypeStruct((3 * PAD, 128), BF16),
        ),
        in_specs=[pl.BlockSpec(memory_space=pltpu.VMEM)] * 2,
        out_specs=(pl.BlockSpec(memory_space=pltpu.VMEM),) * 2,
        scratch_shapes=[
            pltpu.VMEM((2304, 128), F32),
            pltpu.VMEM((2304, 128), F32),
            pltpu.VMEM((320, 128), F32),
            pltpu.VMEM((320, 128), F32),
        ],
        compiler_params=pltpu.CompilerParams(vmem_limit_bytes=VMEM_LIMIT),
        cost_estimate=pl.CostEstimate(flops=2 * 2528 * 256 * 256, bytes_accessed=4000000, transcendentals=0),
    )(fields, north)


OVER_ROWS = (((0,), (0,)), ((), ()))
OVER_LANES = (((1,), (1,)), ((), ()))


def rows_of(b):
    return pl.ds(pl.multiple_of(b * 128, 128), 128)


def vmem_call(kernel, out_shape, scratch, flops, size, *operands, smem=0):
    vmem = pl.BlockSpec(memory_space=pltpu.VMEM)
    scalar = pl.BlockSpec(memory_space=pltpu.SMEM)
    return pl.pallas_call(
        kernel,
        out_shape=out_shape,
        in_specs=[scalar] * smem + [vmem] * (len(operands) - smem),
        out_specs=tuple(vmem for _ in out_shape),
        scratch_shapes=scratch,
        compiler_params=pltpu.CompilerParams(vmem_limit_bytes=VMEM_LIMIT),
        cost_estimate=pl.CostEstimate(flops=flops, bytes_accessed=size, transcendentals=0),
    )(*operands)


def encode_kernel(z_ref, weight_ref, latent_ref, wt, wf):
    for a in range(3):
        wf[...] = jnp.zeros(wf.shape, F32)
        for b in range(3):
            wf[b * PAD:b * PAD + CIN, :] = weight_ref[3 * a + b].astype(F32)
        wt[a] = wf[...].T.astype(BF16)

    def encode_step(k, carry):
        rows = pl.ds(pl.multiple_of(k * 2 * PAD, 16), 3 * PAD)
        total = dot(wt[0], z_ref[0, rows, :])
        total += dot(wt[1], z_ref[1, rows, :])
        total += dot(wt[2], z_ref[2, rows, :])
        latent_ref[pl.ds(k, COUT, stride=16), :] = total
        return carry

    lax.fori_loop(0, 16, encode_step, 0)


def encode(z, weight):
    return vmem_call(
        encode_kernel,
        (jax.ShapeDtypeStruct((WIDTH, TOK), F32),),
        [pltpu.VMEM((3, COUT, 3 * PAD), BF16), pltpu.VMEM((3 * PAD, COUT), F32)],
        2 * 720 * 256 * 2048, 4 * 10**6, z, weight,
    )[0]


def first_column(east_ref, west_ref, a):
    lane = lax.broadcasted_iota(jnp.int32, (PAD, 128), 1)
    own = pltpu.roll(east_ref[a * PAD:(a + 1) * PAD, :].astype(F32), 1, 1)
    other = pltpu.roll(west_ref[a * PAD:(a + 1) * PAD, :].astype(F32), 128 - 7, 1)
    return jnp.where((lane & 7) == 0, other, own).astype(BF16)


def hot_codes(codes_ref, t):
    code = lax.broadcasted_iota(jnp.int32, (NCODE, TOK), 0)
    return (code == codes_ref[t:t + 1, :]).astype(BF16)


def operator_step(coords_ref, low_first, own_ref, other_ref, pull_from, push_from, aa, sa):
    def body(group, carry):
        items = []
        for u in range(UNROLL):
            n = group * UNROLL + u
            i, j = coords_ref[n, 0], coords_ref[n, 1]
            own, other = own_ref[n, 0:64, :], other_ref[n, 0:64, :]
            block = jnp.concatenate(
                [jnp.where(low_first, own, other), jnp.where(low_first, other, own)], axis=0
            )
            items.append((i, j, dot(pull_from(j), block), dot(block, push_from(i))))
        for i, j, pulled, pushed in items:
            aa[i] = aa[i] + pulled
            sa[rows_of(j), :] = sa[rows_of(j), :] + pushed
        return carry

    lax.fori_loop(0, NNZ // UNROLL, body, 0)


UNROLL = 8


def first_kernel(
    coords_ref, core_ref, own_ref, other_ref, latent_ref, east_ref, west_ref, weight_ref,
    table_ref, codes_ref, cot_ref,
    state_ref, adjoint_ref, keep_ref, send_ref,
    sa, sb, aa, ab, wf,
):
    low_first = core_ref[0] == 0
    extra = jnp.zeros((COUT, TOK), F32)
    wf[...] = jnp.zeros(wf.shape, F32)
    for a in range(3):
        wf[0:CIN, :] = weight_ref[3 * a].astype(F32)
        extra += lax.dot_general(
            wf[...].astype(BF16), first_column(east_ref, west_ref, a), OVER_ROWS,
            preferred_element_type=F32,
        )
    sa[...] = latent_ref[...]
    at = pl.ds(0, COUT, stride=16)
    sa[at, :] = sa[at, :] + extra
    hot = hot_codes(codes_ref, 0)

    def begin(b, carry):
        rows = rows_of(b)
        state = sa[rows, :].astype(BF16)
        sb[rows, 0:128] = state
        forcing = lax.dot_general(table_ref[:, rows], hot, OVER_ROWS, preferred_element_type=F32)
        sa[rows, :] = state.astype(F32) + forcing
        cot = cot_ref[:, rows]
        ab[b, 128:256, :] = cot
        aa[b] = cot.astype(F32)
        return carry

    lax.fori_loop(0, NBLK, begin, 0)
    operator_step(
        coords_ref, low_first, own_ref, other_ref,
        lambda j: ab[j, 128:256, :], lambda i: sb[rows_of(i), 0:128], aa, sa,
    )

    def end(b, carry):
        rows = rows_of(b)
        state = sa[rows, :].astype(BF16)
        sb[rows, 128:256] = state
        state_ref[rows, :] = state
        adjoint = aa[b].astype(BF16)
        ab[b, 0:128, :] = adjoint
        adjoint_ref[b] = adjoint
        return carry

    lax.fori_loop(0, NBLK, end, 0)

    def block_grads(group, carry):
        for u in range(UNROLL):
            n = group * UNROLL + u
            i, j = coords_ref[n, 0], coords_ref[n, 1]
            grad = dot(sb[rows_of(i), :], ab[j])
            low, high = grad[0:64], grad[64:128]
            keep = jnp.where(low_first, low, high)
            send = jnp.where(low_first, high, low).astype(BF16)
            for x in range(2):
                keep_ref[x, n] = keep[x * 32:(x + 1) * 32]
                send_ref[x, n] = send[x * 32:(x + 1) * 32]
        return carry

    lax.fori_loop(0, NNZ // UNROLL, block_grads, 0)


def run_first(coords, core, own, other, latent, east, west, weight, table, codes, cot):
    return vmem_call(
        first_kernel,
        (
            jax.ShapeDtypeStruct((WIDTH, TOK), BF16),
            jax.ShapeDtypeStruct((NBLK, TOK, 128), BF16),
            jax.ShapeDtypeStruct((2, NNZ, 32, 128), F32),
            jax.ShapeDtypeStruct((2, NNZ, 32, 128), BF16),
        ),
        [
            pltpu.VMEM((WIDTH, TOK), F32),
            pltpu.VMEM((WIDTH, 2 * TOK), BF16),
            pltpu.VMEM((NBLK, TOK, 128), F32),
            pltpu.VMEM((NBLK, 2 * TOK, 128), BF16),
            pltpu.VMEM((PAD, COUT), F32),
        ],
        10**9, 12 * 10**6,
        coords, core, own, other, latent, east, west, weight, table, codes, cot, smem=2,
    )


def second_kernel(
    coords_ref, core_ref, own_ref, other_ref, state_ref, adjoint_ref, z_ref, east_ref, west_ref,
    table_ref, codes_ref, cot_ref,
    next_ref, out_ref,
    sa, aa, at0, gc, left,
):
    low_first = core_ref[0] == 0
    hot0, hot1 = hot_codes(codes_ref, 0), hot_codes(codes_ref, 1)

    def begin(b, carry):
        rows = rows_of(b)
        forcing = lax.dot_general(table_ref[:, rows], hot1, OVER_ROWS, preferred_element_type=F32)
        sa[rows, :] = state_ref[rows, :].astype(F32) + forcing
        aa[b] = adjoint_ref[b].astype(F32)
        return carry

    lax.fori_loop(0, NBLK, begin, 0)
    operator_step(
        coords_ref, low_first, own_ref, other_ref,
        lambda j: adjoint_ref[j], lambda i: state_ref[rows_of(i), :], aa, sa,
    )

    def end(b, carry):
        rows = rows_of(b)
        next_ref[:, rows] = sa[rows, :].T.astype(BF16)
        at0[rows, :] = aa[b].T
        return carry

    lax.fori_loop(0, NBLK, end, 0)

    for j in range(NBLK):
        term = dot(hot0, adjoint_ref[j]) + dot(hot1, cot_ref[:, j * 128:(j + 1) * 128])
        for third in range(3):
            out_ref[3 * j + third] = term[third * 8:(third + 1) * 8, :]

    gc[...] = jnp.zeros(gc.shape, F32)

    def conv_grads(k, carry):
        adjoint = at0[pl.ds(k, COUT, stride=16), :].astype(BF16)
        rows = pl.ds(pl.multiple_of(k * 2 * PAD, 16), 3 * PAD)
        for a in range(3):
            gc[a] = gc[a] + lax.dot_general(
                z_ref[a, rows, :], adjoint, OVER_LANES, preferred_element_type=F32
            )
        return carry

    lax.fori_loop(0, 16, conv_grads, 0)
    adjoint = at0[pl.ds(0, COUT, stride=16), :].astype(BF16)
    for a in range(3):
        gc[a, 0:PAD, :] = gc[a, 0:PAD, :] + lax.dot_general(
            first_column(east_ref, west_ref, a), adjoint, OVER_LANES, preferred_element_type=F32
        )
    left[...] = jnp.zeros(left.shape, F32)
    for tap in range(9):
        a, b = divmod(tap, 3)
        for half in range(2):
            lanes = slice(half * 128, (half + 1) * 128)
            for g in range(8):
                out_ref[96 + (tap * 8 + g) * 2 + half] = (
                    gc[a, b * PAD + g * 8:b * PAD + g * 8 + 8, lanes]
                )
            at = 5 * (2 * tap + half)
            left[at:at + 5, :] = gc[a, b * PAD + 64:b * PAD + CIN, lanes]
    for m in range(16):
        out_ref[240 + m] = left[m * 8:(m + 1) * 8, :]


def run_second(coords, core, own, other, state, adjoint, z, east, west, table, codes, cot):
    return vmem_call(
        second_kernel,
        (
            jax.ShapeDtypeStruct((TOK, WIDTH), BF16),
            jax.ShapeDtypeStruct((256, 8, 128), F32),
        ),
        [
            pltpu.VMEM((WIDTH, TOK), F32),
            pltpu.VMEM((NBLK, TOK, 128), F32),
            pltpu.VMEM((WIDTH, TOK), F32),
            pltpu.VMEM((3, 3 * PAD, COUT), F32),
            pltpu.VMEM((128, 128), F32),
        ],
        2 * 10**9, 12 * 10**6,
        coords, core, own, other, state, adjoint, z, east, west, table, codes, cot, smem=2,
    )


def unpack_kernel(sums_ref, conv_ref, forcing_ref, left):
    for j in range(NBLK):
        for third in range(3):
            forcing_ref[third * 8:(third + 1) * 8, j * 128:(j + 1) * 128] = sums_ref[3 * j + third]
    for m in range(12):
        left[m * 8:(m + 1) * 8, :] = sums_ref[240 + m]
    for tap in range(9):
        for half in range(2):
            lanes = slice(half * 128, (half + 1) * 128)
            for g in range(8):
                conv_ref[tap, g * 8:(g + 1) * 8, lanes] = sums_ref[96 + (tap * 8 + g) * 2 + half]
            at = 5 * (2 * tap + half)
            conv_ref[tap, 64:CIN, lanes] = left[at:at + 5, :]


def unpack(sums):
    vmem = pl.BlockSpec(memory_space=pltpu.VMEM)
    return pl.pallas_call(
        unpack_kernel,
        out_shape=(
            jax.ShapeDtypeStruct((9, CIN, COUT), F32),
            jax.ShapeDtypeStruct((NCODE, WIDTH), F32),
        ),
        in_specs=[vmem],
        out_specs=(vmem, vmem),
        scratch_shapes=[pltpu.VMEM((96, 128), F32)],
        compiler_params=pltpu.CompilerParams(vmem_limit_bytes=VMEM_LIMIT),
    )(sums)


def per_device(
    fields, conv_weight, kernel_blocks, block_coords, forcing_table, forcing_codes, cotangent
):
    core = lax.axis_index("core")
    top = jnp.pad(fields[:, :, 7, :], ((0, 0), (0, PAD - CIN), (0, 0))).reshape(4 * PAD, 256)
    north = lax.ppermute(top, BAND, [(i, i + 1) for i in range(63)])

    turned = kernel_blocks[0].T
    half = jnp.where(core == 0, turned[0:64], turned[64:128])
    marks = jnp.pad(block_coords.astype(BF16), ((0, 7), (0, 126)))
    payload = jnp.concatenate([half, marks], axis=0)
    spread = jnp.broadcast_to(payload[None], (NNZ,) + payload.shape)
    spread, north = lax.optimization_barrier((spread, north))
    own = lax.all_to_all(spread, BAND, 0, 0, tiled=True)
    z, east = make_patches(fields.reshape(-1, 256), north)
    west = lax.ppermute(east, SECTION, [(i, (i + 1) % 4) for i in range(4)])
    latent = encode(z, conv_weight)
    other = lax.ppermute(own, "core", [(0, 1), (1, 0)])
    coords = own[:, 64, 0:2].astype(jnp.int32)
    codes = forcing_codes.reshape(2, TOK)
    cot = cotangent.reshape(TOK, WIDTH)
    which = core.astype(jnp.int32).reshape(1)

    state, adjoint, keep, send = run_first(
        coords, which, own, other, latent, east, west, conv_weight, forcing_table, codes, cot
    )
    received = lax.ppermute(send, "core", [(0, 1), (1, 0)])
    latent_next, partial = run_second(
        coords, which, own, other, state, adjoint, z, east, west, forcing_table, codes, cot
    )
    terms = lax.all_to_all(partial.astype(BF16), ALL, 0, 0, tiled=True)
    chip = (keep + received.astype(F32)).astype(BF16)
    parts = lax.all_to_all(chip.reshape(128, 32, 128), ("xl",) + BAND, 0, 0, tiled=True)
    shared = jnp.sum(terms.astype(F32), axis=0).astype(BF16)
    everyone = lax.all_to_all(
        jnp.broadcast_to(shared[None], (256, 8, 128)), ALL, 0, 0, tiled=True
    )
    grad_conv, grad_forcing = unpack(everyone.astype(F32))
    quarter = jnp.sum(parts.astype(F32), axis=0)
    others = [
        lax.ppermute(quarter, SECTION, [(i, i ^ flip) for i in range(4)]) for flip in (1, 2, 3)
    ]
    section = 2 * lax.axis_index("xl") + core
    quarters = jnp.stack([quarter] + others)
    order = jnp.stack([section ^ (2 * (q % 2) + q // 2) for q in range(4)])
    grad_blocks = jnp.take(quarters, order, axis=0).reshape(1, 128, 128)
    return (latent_next.reshape(cotangent.shape), grad_conv, grad_blocks, grad_forcing)


def solution(mesh):
    fine = Mesh(mesh.devices.reshape(2, 2, 4, 2, 8), ALL)
    return jax.shard_map(
        per_device,
        mesh=fine,
        in_specs=(
            P(None, None, BAND, SECTION),
            P(),
            P(BAND, None, None),
            P(BAND, None),
            P(),
            P(None, None, BAND, SECTION),
            P(None, BAND, SECTION, None),
        ),
        out_specs=(P(None, BAND, SECTION, None), P(), P(BAND, None, None), P()),
        check_vma=False,
    )
```

```python
import jax
import jax.numpy as jnp
from jax import lax
from jax.experimental import pallas as pl
from jax.experimental.pallas import tpu as pltpu
from jax.sharding import Mesh, PartitionSpec as P

BAND = ("y", "xh", "z")
SECTION = ("xl", "core")
ALL = ("xl", "core", "y", "xh", "z")
CIN, COUT, ROWS, PAD = 69, 256, 16, 80
TOK, WIDTH, NBLK, NNZ, NCODE = 128, 4096, 32, 64, 24
F32, BF16 = jnp.float32, jnp.bfloat16
VMEM_LIMIT = 56 * 1024 * 1024


def dot(a, b):
    return jnp.dot(a, b, preferred_element_type=F32)


def patches_kernel(fields_ref, north_ref, z_ref, east_ref, y0, y1, n0, n1):
    row = lax.broadcasted_iota(jnp.int32, (256, 256), 0)
    col = lax.broadcasted_iota(jnp.int32, (256, 256), 1)
    order = (row == (col & 7) * 32 + (col >> 3)).astype(BF16)

    def spread(step, carry):
        rows = pl.ds(pl.multiple_of(step * 368, 16), 368)
        mixed = dot(fields_ref[rows, :], order)
        y0[rows, :] = mixed[:, :128]
        y1[rows, :] = mixed[:, 128:]
        return carry

    lax.fori_loop(0, 6, spread, 0)
    y0[2208:2304, :] = jnp.zeros((96, 128), F32)
    y1[2208:2304, :] = jnp.zeros((96, 128), F32)
    mixed = dot(north_ref[...], order)
    n0[...] = mixed[:, :128]
    n1[...] = mixed[:, 128:]
    lane = lax.broadcasted_iota(jnp.int32, (16, 128), 1)

    def chunk(step, carry):
        for half, (rows_ref, top_ref) in enumerate(((y0, n0), (y1, n1))):
            for a in range(3):
                parts = []
                for s in range(4):
                    for r in range(4):
                        lat = 2 * r + a - 1
                        if lat < 0:
                            at = pl.ds(pl.multiple_of(s * PAD + step * 16, 16), 16)
                            parts.append(top_ref[at, :])
                        else:
                            at = pl.ds(s * CIN * 8 + lat + step * 128, 16, stride=8)
                            parts.append(rows_ref[at, :])
                for bit in (1, 2, 4, 8):
                    high = (lane & (8 * bit)) != 0
                    for i in range(16):
                        if i & bit:
                            continue
                        low_part, high_part = parts[i], parts[i | bit]
                        parts[i] = jnp.where(high, pltpu.roll(high_part, 8 * bit, 1), low_part)
                        parts[i | bit] = jnp.where(
                            high, high_part, pltpu.roll(low_part, 128 - 8 * bit, 1)
                        )
                for q in range(16):
                    at = pl.multiple_of((half * 16 + q + 1) * PAD + step * 16, 16)
                    z_ref[a, pl.ds(at, 16), :] = parts[q].astype(BF16)
                if half == 1:
                    at = pl.multiple_of(a * PAD + step * 16, 16)
                    east_ref[pl.ds(at, 16), :] = parts[15].astype(BF16)
        return carry

    lax.fori_loop(0, PAD // 16, chunk, 0)
    for a in range(3):
        z_ref[a, 0:PAD, :] = jnp.zeros((PAD, 128), BF16)


def make_patches(fields, north):
    return pl.pallas_call(
        patches_kernel,
        out_shape=(
            jax.ShapeDtypeStruct((3, 33 * PAD, 128), BF16),
            jax.ShapeDtypeStruct((3 * PAD, 128), BF16),
        ),
        in_specs=[pl.BlockSpec(memory_space=pltpu.VMEM)] * 2,
        out_specs=(pl.BlockSpec(memory_space=pltpu.VMEM),) * 2,
        scratch_shapes=[
            pltpu.VMEM((2304, 128), F32),
            pltpu.VMEM((2304, 128), F32),
            pltpu.VMEM((320, 128), F32),
            pltpu.VMEM((320, 128), F32),
        ],
        compiler_params=pltpu.CompilerParams(vmem_limit_bytes=VMEM_LIMIT),
        cost_estimate=pl.CostEstimate(flops=2 * 2528 * 256 * 256, bytes_accessed=4000000, transcendentals=0),
    )(fields, north)


OVER_ROWS = (((0,), (0,)), ((), ()))
OVER_LANES = (((1,), (1,)), ((), ()))


def rows_of(b):
    return pl.ds(pl.multiple_of(b * 128, 128), 128)


def vmem_call(kernel, out_shape, scratch, flops, size, *operands, smem=0):
    vmem = pl.BlockSpec(memory_space=pltpu.VMEM)
    scalar = pl.BlockSpec(memory_space=pltpu.SMEM)
    return pl.pallas_call(
        kernel,
        out_shape=out_shape,
        in_specs=[scalar] * smem + [vmem] * (len(operands) - smem),
        out_specs=tuple(vmem for _ in out_shape),
        scratch_shapes=scratch,
        compiler_params=pltpu.CompilerParams(vmem_limit_bytes=VMEM_LIMIT),
        cost_estimate=pl.CostEstimate(flops=flops, bytes_accessed=size, transcendentals=0),
    )(*operands)


def encode_kernel(z_ref, weight_ref, latent_ref, wt, wf):
    for a in range(3):
        wf[...] = jnp.zeros(wf.shape, F32)
        for b in range(3):
            wf[b * PAD:b * PAD + CIN, :] = weight_ref[3 * a + b].astype(F32)
        wt[a] = wf[...].T.astype(BF16)

    def encode_step(k, carry):
        rows = pl.ds(pl.multiple_of(k * 2 * PAD, 16), 3 * PAD)
        total = dot(wt[0], z_ref[0, rows, :])
        total += dot(wt[1], z_ref[1, rows, :])
        total += dot(wt[2], z_ref[2, rows, :])
        latent_ref[pl.ds(k, COUT, stride=16), :] = total
        return carry

    lax.fori_loop(0, 16, encode_step, 0)


def encode(z, weight):
    return vmem_call(
        encode_kernel,
        (jax.ShapeDtypeStruct((WIDTH, TOK), F32),),
        [pltpu.VMEM((3, COUT, 3 * PAD), BF16), pltpu.VMEM((3 * PAD, COUT), F32)],
        2 * 720 * 256 * 2048, 4 * 10**6, z, weight,
    )[0]


def first_column(east_ref, west_ref, a):
    lane = lax.broadcasted_iota(jnp.int32, (PAD, 128), 1)
    own = pltpu.roll(east_ref[a * PAD:(a + 1) * PAD, :].astype(F32), 1, 1)
    other = pltpu.roll(west_ref[a * PAD:(a + 1) * PAD, :].astype(F32), 128 - 7, 1)
    return jnp.where((lane & 7) == 0, other, own).astype(BF16)


def hot_codes(codes_ref, t):
    code = lax.broadcasted_iota(jnp.int32, (NCODE, TOK), 0)
    return (code == codes_ref[t:t + 1, :]).astype(BF16)


def block_of(n, low_first, own_ref, other_ref):
    own, other = own_ref[n, 0:64, :], other_ref[n, 0:64, :]
    return jnp.concatenate(
        [jnp.where(low_first, own, other), jnp.where(low_first, other, own)], axis=0
    )


def pull(coords_ref, low_first, own_ref, other_ref, source, target):
    def body(group, carry):
        items = []
        for u in range(UNROLL):
            n = group * UNROLL + u
            block = block_of(n, low_first, own_ref, other_ref)
            items.append((coords_ref[n, 0], dot(source(coords_ref[n, 1]), block)))
        for i, term in items:
            target[i] = target[i] + term
        return carry

    lax.fori_loop(0, NNZ // UNROLL, body, 0)


def push(coords_ref, low_first, own_ref, other_ref, source, target):
    def body(group, carry):
        items = []
        for u in range(UNROLL):
            n = group * UNROLL + u
            block = block_of(n, low_first, own_ref, other_ref)
            items.append((coords_ref[n, 1], dot(block, source(coords_ref[n, 0]))))
        for j, term in items:
            target[rows_of(j), :] = target[rows_of(j), :] + term
        return carry

    lax.fori_loop(0, NNZ // UNROLL, body, 0)


UNROLL = 8


def adjoint_kernel(
    coords_ref, core_ref, own_ref, other_ref, z_ref, east_ref, west_ref, codes_ref, cot_ref,
    adjoint_ref, out_ref,
    later, sums, turned, gc, left,
):
    low_first = core_ref[0] == 0
    for b in range(NBLK):
        cot = cot_ref[:, b * 128:(b + 1) * 128]
        later[b] = cot
        sums[b] = cot.astype(F32)
    pull(coords_ref, low_first, own_ref, other_ref, lambda j: later[j], sums)

    def between(b, carry):
        adjoint = sums[b].astype(BF16)
        adjoint_ref[b] = adjoint
        sums[b] = adjoint.astype(F32)
        return carry

    lax.fori_loop(0, NBLK, between, 0, unroll=4)
    pull(coords_ref, low_first, own_ref, other_ref, lambda j: adjoint_ref[j], sums)

    def end(b, carry):
        turned[rows_of(b), :] = sums[b].T
        return carry

    lax.fori_loop(0, NBLK, end, 0, unroll=4)
    hot = jnp.concatenate([hot_codes(codes_ref, 0), hot_codes(codes_ref, 1)], axis=1)
    for j in range(NBLK):
        both = jnp.concatenate([adjoint_ref[j], later[j]], axis=0)
        term = dot(hot, both).astype(BF16)
        for third in range(3):
            out_ref[3 * j + third] = term[third * 8:(third + 1) * 8, :]

    def conv_grads(pair, carry):
        adjoint, rows = [], []
        for u in range(2):
            k = 2 * pair + u
            adjoint.append(turned[pl.ds(k, COUT, stride=16), :].astype(BF16))
            rows.append(pl.ds(pl.multiple_of(k * 2 * PAD, 16), 3 * PAD))
        adjoint = jnp.concatenate(adjoint, axis=1)
        for a in range(3):
            patches = jnp.concatenate([z_ref[a, rows[0], :], z_ref[a, rows[1], :]], axis=1)
            gc[a] = gc[a] + lax.dot_general(
                patches, adjoint, OVER_LANES, preferred_element_type=F32
            )
        return carry

    gc[...] = jnp.zeros(gc.shape, F32)
    adjoint = turned[pl.ds(0, COUT, stride=16), :].astype(BF16)
    for a in range(3):
        gc[a, 0:PAD, :] = lax.dot_general(
            first_column(east_ref, west_ref, a), adjoint, OVER_LANES, preferred_element_type=F32
        )
    lax.fori_loop(0, 8, conv_grads, 0)
    left[...] = jnp.zeros(left.shape, F32)
    for tap in range(9):
        a, b = divmod(tap, 3)
        for half in range(2):
            lanes = slice(half * 128, (half + 1) * 128)
            for g in range(8):
                out_ref[96 + (tap * 8 + g) * 2 + half] = (
                    gc[a, b * PAD + g * 8:b * PAD + g * 8 + 8, lanes].astype(BF16)
                )
            at = 5 * (2 * tap + half)
            left[at:at + 5, :] = gc[a, b * PAD + 64:b * PAD + CIN, lanes]
    for m in range(16):
        out_ref[240 + m] = left[m * 8:(m + 1) * 8, :].astype(BF16)


def run_adjoint(coords, core, own, other, z, east, west, codes, cot):
    return vmem_call(
        adjoint_kernel,
        (
            jax.ShapeDtypeStruct((NBLK, TOK, 128), BF16),
            jax.ShapeDtypeStruct((256, 8, 128), BF16),
        ),
        [
            pltpu.VMEM((NBLK, TOK, 128), BF16),
            pltpu.VMEM((NBLK, TOK, 128), F32),
            pltpu.VMEM((WIDTH, TOK), F32),
            pltpu.VMEM((3, 3 * PAD, COUT), F32),
            pltpu.VMEM((128, 128), F32),
        ],
        1500 * 10**6, 8 * 10**6,
        coords, core, own, other, z, east, west, codes, cot, smem=2,
    )


def forward_kernel(
    coords_ref, core_ref, own_ref, other_ref, latent_ref, east_ref, west_ref, weight_ref,
    table_ref, codes_ref, adjoint_ref, cot_ref,
    state_ref, keep_ref, send_ref,
    sums, states, adjoints, wf,
):
    low_first = core_ref[0] == 0
    extra = jnp.zeros((COUT, TOK), F32)
    wf[...] = jnp.zeros(wf.shape, F32)
    for a in range(3):
        wf[0:CIN, :] = weight_ref[3 * a].astype(F32)
        extra += lax.dot_general(
            wf[...].astype(BF16), first_column(east_ref, west_ref, a), OVER_ROWS,
            preferred_element_type=F32,
        )
    at = pl.ds(0, COUT, stride=16)
    sums[...] = latent_ref[...]
    sums[at, :] = sums[at, :] + extra
    hot = hot_codes(codes_ref, 0)
    for b in range(NBLK):
        rows = slice(b * 128, (b + 1) * 128)
        state = sums[rows, :].astype(BF16)
        states[rows, 0:128] = state
        forcing = lax.dot_general(table_ref[:, rows], hot, OVER_ROWS, preferred_element_type=F32)
        sums[rows, :] = state.astype(F32) + forcing
        adjoints[b, 0:128, :] = adjoint_ref[b]
        adjoints[b, 128:256, :] = cot_ref[:, rows]
    push(
        coords_ref, low_first, own_ref, other_ref,
        lambda i: states[rows_of(i), 0:128], sums,
    )

    def end(b, carry):
        rows = rows_of(b)
        state = sums[rows, :].astype(BF16)
        states[rows, 128:256] = state
        state_ref[rows, :] = state
        return carry

    lax.fori_loop(0, NBLK, end, 0, unroll=4)

    def block_grads(group, carry):
        for u in range(UNROLL):
            n = group * UNROLL + u
            i, j = coords_ref[n, 0], coords_ref[n, 1]
            grad = dot(states[rows_of(i), :], adjoints[j])
            low, high = grad[0:64], grad[64:128]
            keep = jnp.where(low_first, low, high)
            send = jnp.where(low_first, high, low).astype(BF16)
            for x in range(2):
                keep_ref[x, n] = keep[x * 32:(x + 1) * 32]
                send_ref[x, n] = send[x * 32:(x + 1) * 32]
        return carry

    lax.fori_loop(0, NNZ // UNROLL, block_grads, 0)


def run_forward(coords, core, own, other, latent, east, west, weight, table, codes, adjoint, cot):
    return vmem_call(
        forward_kernel,
        (
            jax.ShapeDtypeStruct((WIDTH, TOK), BF16),
            jax.ShapeDtypeStruct((2, NNZ, 32, 128), F32),
            jax.ShapeDtypeStruct((2, NNZ, 32, 128), BF16),
        ),
        [
            pltpu.VMEM((WIDTH, TOK), F32),
            pltpu.VMEM((WIDTH, 2 * TOK), BF16),
            pltpu.VMEM((NBLK, 2 * TOK, 128), BF16),
            pltpu.VMEM((PAD, COUT), F32),
        ],
        1000, 1000,
        coords, core, own, other, latent, east, west, weight, table, codes, adjoint, cot, smem=2,
    )


def last_kernel(
    coords_ref, core_ref, own_ref, other_ref, state_ref, table_ref, codes_ref, next_ref, sums,
):
    low_first = core_ref[0] == 0
    hot = hot_codes(codes_ref, 1)
    for b in range(NBLK):
        rows = slice(b * 128, (b + 1) * 128)
        forcing = lax.dot_general(table_ref[:, rows], hot, OVER_ROWS, preferred_element_type=F32)
        sums[rows, :] = state_ref[rows, :].astype(F32) + forcing
    push(coords_ref, low_first, own_ref, other_ref, lambda i: state_ref[rows_of(i), :], sums)
    for b in range(NBLK):
        rows = slice(b * 128, (b + 1) * 128)
        next_ref[:, rows] = sums[rows, :].T.astype(BF16)


def run_last(coords, core, own, other, state, table, codes):
    return vmem_call(
        last_kernel,
        (jax.ShapeDtypeStruct((TOK, WIDTH), BF16),),
        [pltpu.VMEM((WIDTH, TOK), F32)],
        1000, 1000,
        coords, core, own, other, state, table, codes, smem=2,
    )[0]


def unpack_kernel(plane_ref, conv_ref, forcing_ref, left):
    tiles = {}
    for p in range(16):
        for pair in range(8):
            rows = plane_ref[p, 256 + pair * 16:256 + pair * 16 + 16, :].astype(F32)
            for z in range(2):
                xl, yx = divmod(p, 8)
                core, pair_z = divmod(pair, 4)
                m = xl * 128 + core * 64 + yx * 8 + pair_z * 2 + z
                tiles[m] = rows[z * 8:z * 8 + 8]
    for j in range(NBLK):
        for third in range(3):
            forcing_ref[third * 8:(third + 1) * 8, j * 128:(j + 1) * 128] = tiles[3 * j + third]
    for m in range(12):
        left[m * 8:(m + 1) * 8, :] = tiles[240 + m]
    for tap in range(9):
        for half in range(2):
            lanes = slice(half * 128, (half + 1) * 128)
            for g in range(8):
                conv_ref[tap, g * 8:(g + 1) * 8, lanes] = tiles[96 + (tap * 8 + g) * 2 + half]
            at = 5 * (2 * tap + half)
            conv_ref[tap, 64:CIN, lanes] = left[at:at + 5, :]


def unpack(plane):
    return vmem_call(
        unpack_kernel,
        (
            jax.ShapeDtypeStruct((9, CIN, COUT), F32),
            jax.ShapeDtypeStruct((NCODE, WIDTH), F32),
        ),
        [pltpu.VMEM((96, 128), F32)],
        1000, 3 * 10**6, plane,
    )


def per_device(
    fields, conv_weight, kernel_blocks, block_coords, forcing_table, forcing_codes, cotangent
):
    core = lax.axis_index("core")
    top = jnp.pad(fields[:, :, 7, :], ((0, 0), (0, PAD - CIN), (0, 0))).reshape(4 * PAD, 256)

    turned = kernel_blocks[0].T
    half = jnp.where(core == 0, turned[0:64], turned[64:128])
    marks = jnp.pad(block_coords.astype(BF16), ((0, 7), (0, 126)))
    payload = jnp.concatenate([half, marks], axis=0)
    north = lax.ppermute(top, BAND, [(i, i + 1) for i in range(63)])
    column = lax.all_to_all(
        jnp.broadcast_to(payload[None], (8,) + payload.shape), "z", 0, 0, tiled=True
    )
    column, north = lax.optimization_barrier((column, north))
    own = lax.all_to_all(
        jnp.broadcast_to(column[None], (8,) + column.shape), ("y", "xh"), 0, 0, tiled=True
    ).reshape((NNZ,) + payload.shape)
    z, east = make_patches(fields.reshape(-1, 256), north)
    west = lax.ppermute(east, SECTION, [(i, (i + 1) % 4) for i in range(4)])
    latent = encode(z, conv_weight)
    own, latent = lax.optimization_barrier((own, latent))
    other = lax.ppermute(own, "core", [(0, 1), (1, 0)])
    coords = own[:, 64, 0:2].astype(jnp.int32)
    codes = forcing_codes.reshape(2, TOK)
    cot = cotangent.reshape(TOK, WIDTH)
    which = core.astype(jnp.int32).reshape(1)

    adjoint, partial = run_adjoint(coords, which, own, other, z, east, west, codes, cot)
    terms = lax.all_to_all(partial, ALL, 0, 0, tiled=True)
    state, keep, send = run_forward(
        coords, which, own, other, latent, east, west, conv_weight, forcing_table, codes,
        adjoint, cot,
    )
    received = lax.ppermute(send, "core", [(0, 1), (1, 0)])
    latent_next = run_last(coords, which, own, other, state, forcing_table, codes)
    shared = jnp.sum(terms.astype(F32), axis=0).astype(BF16)
    column = lax.all_to_all(
        jnp.broadcast_to(shared[None], (16, 8, 128)), ("core", "z"), 0, 0, tiled=True
    ).reshape(128, 128)
    column, received, latent_next = lax.optimization_barrier((column, received, latent_next))
    chip = (keep + received.astype(F32)).astype(BF16).reshape(16, 256, 128)
    plane = lax.all_to_all(
        jnp.concatenate([chip, jnp.broadcast_to(column[None], (16, 128, 128))], axis=1),
        ("xl", "y", "xh"), 0, 0, tiled=True,
    )
    grad_conv, grad_forcing = unpack(plane)
    quarter = jnp.sum(plane[:, 0:256].astype(F32), axis=0).astype(BF16).reshape(8, 32, 128)
    parts = lax.all_to_all(
        jnp.broadcast_to(quarter[None], (4, 8, 32, 128)).reshape(32, 32, 128),
        ("xl", "core", "z"), 0, 0, tiled=True,
    )
    quarters = jnp.sum(parts.reshape(2, 2, 8, 32, 128).astype(F32), axis=2)
    grad_blocks = jnp.transpose(quarters, (1, 0, 2, 3)).reshape(1, 128, 128)
    return (latent_next.reshape(cotangent.shape), grad_conv, grad_blocks, grad_forcing)


def solution(mesh):
    fine = Mesh(mesh.devices.reshape(2, 2, 4, 2, 8), ALL)
    return jax.shard_map(
        per_device,
        mesh=fine,
        in_specs=(
            P(None, None, BAND, SECTION),
            P(),
            P(BAND, None, None),
            P(BAND, None),
            P(),
            P(None, None, BAND, SECTION),
            P(None, BAND, SECTION, None),
        ),
        out_specs=(P(None, BAND, SECTION, None), P(), P(BAND, None, None), P()),
        check_vma=False,
    )
```

```python
import jax
import jax.numpy as jnp
from jax import lax
from jax.experimental import pallas as pl
from jax.experimental.pallas import tpu as pltpu
from jax.sharding import Mesh, PartitionSpec as P

BAND = ("y", "xh", "z")
SECTION = ("xl", "core")
ALL = ("xl", "core", "y", "xh", "z")
CIN, COUT, ROWS, PAD = 69, 256, 16, 80
TOK, WIDTH, NBLK, NNZ, NCODE = 128, 4096, 32, 64, 24
F32, BF16 = jnp.float32, jnp.bfloat16
VMEM_LIMIT = 56 * 1024 * 1024


def dot(a, b):
    return jnp.dot(a, b, preferred_element_type=F32)


def patches_kernel(fields_ref, north_ref, z_ref, east_ref, y0, y1, n0, n1):
    row = lax.broadcasted_iota(jnp.int32, (256, 256), 0)
    col = lax.broadcasted_iota(jnp.int32, (256, 256), 1)
    order = (row == (col & 7) * 32 + (col >> 3)).astype(BF16)

    def spread(step, carry):
        rows = pl.ds(pl.multiple_of(step * 368, 16), 368)
        mixed = dot(fields_ref[rows, :], order)
        y0[rows, :] = mixed[:, :128]
        y1[rows, :] = mixed[:, 128:]
        return carry

    lax.fori_loop(0, 6, spread, 0)
    y0[2208:2304, :] = jnp.zeros((96, 128), F32)
    y1[2208:2304, :] = jnp.zeros((96, 128), F32)
    mixed = dot(north_ref[...], order)
    n0[...] = mixed[:, :128]
    n1[...] = mixed[:, 128:]
    lane = lax.broadcasted_iota(jnp.int32, (16, 128), 1)

    def chunk(step, carry):
        for half, (rows_ref, top_ref) in enumerate(((y0, n0), (y1, n1))):
            for a in range(3):
                parts = []
                for s in range(4):
                    for r in range(4):
                        lat = 2 * r + a - 1
                        if lat < 0:
                            at = pl.ds(pl.multiple_of(s * PAD + step * 16, 16), 16)
                            parts.append(top_ref[at, :])
                        else:
                            at = pl.ds(s * CIN * 8 + lat + step * 128, 16, stride=8)
                            parts.append(rows_ref[at, :])
                for bit in (1, 2, 4, 8):
                    high = (lane & (8 * bit)) != 0
                    for i in range(16):
                        if i & bit:
                            continue
                        low_part, high_part = parts[i], parts[i | bit]
                        parts[i] = jnp.where(high, pltpu.roll(high_part, 8 * bit, 1), low_part)
                        parts[i | bit] = jnp.where(
                            high, high_part, pltpu.roll(low_part, 128 - 8 * bit, 1)
                        )
                for q in range(16):
                    at = pl.multiple_of((half * 16 + q + 1) * PAD + step * 16, 16)
                    z_ref[a, pl.ds(at, 16), :] = parts[q].astype(BF16)
                if half == 1:
                    at = pl.multiple_of(a * PAD + step * 16, 16)
                    east_ref[pl.ds(at, 16), :] = parts[15].astype(BF16)
        return carry

    lax.fori_loop(0, PAD // 16, chunk, 0)
    for a in range(3):
        z_ref[a, 0:PAD, :] = jnp.zeros((PAD, 128), BF16)


def make_patches(fields, north):
    return pl.pallas_call(
        patches_kernel,
        out_shape=(
            jax.ShapeDtypeStruct((3, 33 * PAD, 128), BF16),
            jax.ShapeDtypeStruct((3 * PAD, 128), BF16),
        ),
        in_specs=[pl.BlockSpec(memory_space=pltpu.VMEM)] * 2,
        out_specs=(pl.BlockSpec(memory_space=pltpu.VMEM),) * 2,
        scratch_shapes=[
            pltpu.VMEM((2304, 128), F32),
            pltpu.VMEM((2304, 128), F32),
            pltpu.VMEM((320, 128), F32),
            pltpu.VMEM((320, 128), F32),
        ],
        compiler_params=pltpu.CompilerParams(vmem_limit_bytes=VMEM_LIMIT),
        cost_estimate=pl.CostEstimate(flops=2 * 2528 * 256 * 256, bytes_accessed=4000000, transcendentals=0),
    )(fields, north)


OVER_ROWS = (((0,), (0,)), ((), ()))
OVER_LANES = (((1,), (1,)), ((), ()))


def rows_of(b):
    return pl.ds(pl.multiple_of(b * 128, 128), 128)


def vmem_call(kernel, out_shape, scratch, flops, size, *operands, smem=0):
    vmem = pl.BlockSpec(memory_space=pltpu.VMEM)
    scalar = pl.BlockSpec(memory_space=pltpu.SMEM)
    return pl.pallas_call(
        kernel,
        out_shape=out_shape,
        in_specs=[scalar] * smem + [vmem] * (len(operands) - smem),
        out_specs=tuple(vmem for _ in out_shape),
        scratch_shapes=scratch,
        compiler_params=pltpu.CompilerParams(vmem_limit_bytes=VMEM_LIMIT),
        cost_estimate=pl.CostEstimate(flops=flops, bytes_accessed=size, transcendentals=0),
    )(*operands)


def encode_kernel(z_ref, weight_ref, latent_ref, wt, wf):
    for a in range(3):
        wf[...] = jnp.zeros(wf.shape, F32)
        for b in range(3):
            wf[b * PAD:b * PAD + CIN, :] = weight_ref[3 * a + b].astype(F32)
        wt[a] = wf[...].T.astype(BF16)

    def encode_step(k, carry):
        rows = pl.ds(pl.multiple_of(k * 2 * PAD, 16), 3 * PAD)
        total = dot(wt[0], z_ref[0, rows, :])
        total += dot(wt[1], z_ref[1, rows, :])
        total += dot(wt[2], z_ref[2, rows, :])
        latent_ref[pl.ds(k, COUT, stride=16), :] = total
        return carry

    lax.fori_loop(0, 16, encode_step, 0)


def encode(z, weight):
    return vmem_call(
        encode_kernel,
        (jax.ShapeDtypeStruct((WIDTH, TOK), F32),),
        [pltpu.VMEM((3, COUT, 3 * PAD), BF16), pltpu.VMEM((3 * PAD, COUT), F32)],
        2 * 720 * 256 * 2048, 4 * 10**6, z, weight,
    )[0]


def first_column(east_ref, west_ref, a):
    lane = lax.broadcasted_iota(jnp.int32, (PAD, 128), 1)
    own = pltpu.roll(east_ref[a * PAD:(a + 1) * PAD, :].astype(F32), 1, 1)
    other = pltpu.roll(west_ref[a * PAD:(a + 1) * PAD, :].astype(F32), 128 - 7, 1)
    return jnp.where((lane & 7) == 0, other, own).astype(BF16)


def hot_codes(codes_ref, t):
    code = lax.broadcasted_iota(jnp.int32, (NCODE, TOK), 0)
    return (code == codes_ref[t:t + 1, :]).astype(BF16)


def block_of(n, low_first, own_ref, other_ref):
    own, other = own_ref[n, 0:64, :], other_ref[n, 0:64, :]
    return jnp.concatenate(
        [jnp.where(low_first, own, other), jnp.where(low_first, other, own)], axis=0
    )


def pull(coords_ref, low_first, own_ref, other_ref, source, target):
    def body(group, carry):
        items = []
        for u in range(UNROLL):
            n = group * UNROLL + u
            block = block_of(n, low_first, own_ref, other_ref)
            items.append((coords_ref[n, 0], dot(source(coords_ref[n, 1]), block)))
        for i, term in items:
            target[i] = target[i] + term
        return carry

    lax.fori_loop(0, NNZ // UNROLL, body, 0)


def push(coords_ref, low_first, own_ref, other_ref, source, target):
    def body(group, carry):
        items = []
        for u in range(UNROLL):
            n = group * UNROLL + u
            block = block_of(n, low_first, own_ref, other_ref)
            items.append((coords_ref[n, 1], dot(block, source(coords_ref[n, 0]))))
        for j, term in items:
            target[rows_of(j), :] = target[rows_of(j), :] + term
        return carry

    lax.fori_loop(0, NNZ // UNROLL, body, 0)


UNROLL = 8


def adjoint_kernel(
    coords_ref, core_ref, own_ref, other_ref, z_ref, east_ref, west_ref, codes_ref, cot_ref,
    adjoint_ref, out_ref,
    later, sums, turned, gc, left,
):
    low_first = core_ref[0] == 0
    for b in range(NBLK):
        cot = cot_ref[:, b * 128:(b + 1) * 128]
        later[b] = cot
        sums[b] = cot.astype(F32)
    pull(coords_ref, low_first, own_ref, other_ref, lambda j: later[j], sums)

    def between(b, carry):
        adjoint = sums[b].astype(BF16)
        adjoint_ref[b] = adjoint
        sums[b] = adjoint.astype(F32)
        return carry

    lax.fori_loop(0, NBLK, between, 0, unroll=4)
    pull(coords_ref, low_first, own_ref, other_ref, lambda j: adjoint_ref[j], sums)

    def end(b, carry):
        turned[rows_of(b), :] = sums[b].T
        return carry

    lax.fori_loop(0, NBLK, end, 0, unroll=4)
    hot = jnp.concatenate([hot_codes(codes_ref, 0), hot_codes(codes_ref, 1)], axis=1)
    for j in range(NBLK):
        both = jnp.concatenate([adjoint_ref[j], later[j]], axis=0)
        term = dot(hot, both).astype(BF16)
        for third in range(3):
            out_ref[3 * j + third] = term[third * 8:(third + 1) * 8, :]

    def conv_grads(pair, carry):
        adjoint, rows = [], []
        for u in range(2):
            k = 2 * pair + u
            adjoint.append(turned[pl.ds(k, COUT, stride=16), :].astype(BF16))
            rows.append(pl.ds(pl.multiple_of(k * 2 * PAD, 16), 3 * PAD))
        adjoint = jnp.concatenate(adjoint, axis=1)
        for a in range(3):
            patches = jnp.concatenate([z_ref[a, rows[0], :], z_ref[a, rows[1], :]], axis=1)
            gc[a] = gc[a] + lax.dot_general(
                patches, adjoint, OVER_LANES, preferred_element_type=F32
            )
        return carry

    gc[...] = jnp.zeros(gc.shape, F32)
    adjoint = turned[pl.ds(0, COUT, stride=16), :].astype(BF16)
    for a in range(3):
        gc[a, 0:PAD, :] = lax.dot_general(
            first_column(east_ref, west_ref, a), adjoint, OVER_LANES, preferred_element_type=F32
        )
    lax.fori_loop(0, 8, conv_grads, 0)
    left[...] = jnp.zeros(left.shape, F32)
    for tap in range(9):
        a, b = divmod(tap, 3)
        for half in range(2):
            lanes = slice(half * 128, (half + 1) * 128)
            for g in range(8):
                out_ref[96 + (tap * 8 + g) * 2 + half] = (
                    gc[a, b * PAD + g * 8:b * PAD + g * 8 + 8, lanes].astype(BF16)
                )
            at = 5 * (2 * tap + half)
            left[at:at + 5, :] = gc[a, b * PAD + 64:b * PAD + CIN, lanes]
    for m in range(16):
        out_ref[240 + m] = left[m * 8:(m + 1) * 8, :].astype(BF16)


def run_adjoint(coords, core, own, other, z, east, west, codes, cot):
    return vmem_call(
        adjoint_kernel,
        (
            jax.ShapeDtypeStruct((NBLK, TOK, 128), BF16),
            jax.ShapeDtypeStruct((256, 8, 128), BF16),
        ),
        [
            pltpu.VMEM((NBLK, TOK, 128), BF16),
            pltpu.VMEM((NBLK, TOK, 128), F32),
            pltpu.VMEM((WIDTH, TOK), F32),
            pltpu.VMEM((3, 3 * PAD, COUT), F32),
            pltpu.VMEM((128, 128), F32),
        ],
        1500 * 10**6, 8 * 10**6,
        coords, core, own, other, z, east, west, codes, cot, smem=2,
    )


def forward_kernel(
    coords_ref, core_ref, own_ref, other_ref, latent_ref, east_ref, west_ref, weight_ref,
    table_ref, codes_ref, adjoint_ref, cot_ref,
    state_ref, keep_ref, send_ref,
    sums, states, adjoints, wf,
):
    low_first = core_ref[0] == 0
    extra = jnp.zeros((COUT, TOK), F32)
    wf[...] = jnp.zeros(wf.shape, F32)
    for a in range(3):
        wf[0:CIN, :] = weight_ref[3 * a].astype(F32)
        extra += lax.dot_general(
            wf[...].astype(BF16), first_column(east_ref, west_ref, a), OVER_ROWS,
            preferred_element_type=F32,
        )
    at = pl.ds(0, COUT, stride=16)
    sums[...] = latent_ref[...]
    sums[at, :] = sums[at, :] + extra
    hot = hot_codes(codes_ref, 0)
    for b in range(NBLK):
        rows = slice(b * 128, (b + 1) * 128)
        state = sums[rows, :].astype(BF16)
        states[rows, 0:128] = state
        forcing = lax.dot_general(table_ref[:, rows], hot, OVER_ROWS, preferred_element_type=F32)
        sums[rows, :] = state.astype(F32) + forcing
        adjoints[b, 0:128, :] = adjoint_ref[b]
        adjoints[b, 128:256, :] = cot_ref[:, rows]
    push(
        coords_ref, low_first, own_ref, other_ref,
        lambda i: states[rows_of(i), 0:128], sums,
    )

    def end(b, carry):
        rows = rows_of(b)
        state = sums[rows, :].astype(BF16)
        states[rows, 128:256] = state
        state_ref[rows, :] = state
        return carry

    lax.fori_loop(0, NBLK, end, 0, unroll=4)

    def block_grads(group, carry):
        for u in range(UNROLL):
            n = group * UNROLL + u
            i, j = coords_ref[n, 0], coords_ref[n, 1]
            grad = dot(states[rows_of(i), :], adjoints[j])
            low, high = grad[0:64], grad[64:128]
            keep = jnp.where(low_first, low, high)
            send = jnp.where(low_first, high, low).astype(BF16)
            for x in range(2):
                keep_ref[x, n] = keep[x * 32:(x + 1) * 32]
                send_ref[x, n] = send[x * 32:(x + 1) * 32]
        return carry

    lax.fori_loop(0, NNZ // UNROLL, block_grads, 0)


def run_forward(coords, core, own, other, latent, east, west, weight, table, codes, adjoint, cot):
    return vmem_call(
        forward_kernel,
        (
            jax.ShapeDtypeStruct((WIDTH, TOK), BF16),
            jax.ShapeDtypeStruct((2, NNZ, 32, 128), F32),
            jax.ShapeDtypeStruct((2, NNZ, 32, 128), BF16),
        ),
        [
            pltpu.VMEM((WIDTH, TOK), F32),
            pltpu.VMEM((WIDTH, 2 * TOK), BF16),
            pltpu.VMEM((NBLK, 2 * TOK, 128), BF16),
            pltpu.VMEM((PAD, COUT), F32),
        ],
        1000, 1000,
        coords, core, own, other, latent, east, west, weight, table, codes, adjoint, cot, smem=2,
    )


def last_kernel(
    coords_ref, core_ref, own_ref, other_ref, state_ref, table_ref, codes_ref, next_ref, sums,
):
    low_first = core_ref[0] == 0
    hot = hot_codes(codes_ref, 1)
    for b in range(NBLK):
        rows = slice(b * 128, (b + 1) * 128)
        forcing = lax.dot_general(table_ref[:, rows], hot, OVER_ROWS, preferred_element_type=F32)
        sums[rows, :] = state_ref[rows, :].astype(F32) + forcing
    push(coords_ref, low_first, own_ref, other_ref, lambda i: state_ref[rows_of(i), :], sums)
    for b in range(NBLK):
        rows = slice(b * 128, (b + 1) * 128)
        next_ref[:, rows] = sums[rows, :].T.astype(BF16)


def run_last(coords, core, own, other, state, table, codes):
    return vmem_call(
        last_kernel,
        (jax.ShapeDtypeStruct((TOK, WIDTH), BF16),),
        [pltpu.VMEM((WIDTH, TOK), F32)],
        1000, 1000,
        coords, core, own, other, state, table, codes, smem=2,
    )[0]


def unpack_kernel(core_ref, own_ref, other_ref, conv_ref, forcing_ref, left):
    low_first = core_ref[0] == 0
    tiles = {}
    for p in range(16):
        for pair in range(4):
            own = own_ref[p, pair * 16:pair * 16 + 16, :].astype(F32)
            other = other_ref[p, pair * 16:pair * 16 + 16, :].astype(F32)
            both = (jnp.where(low_first, own, other), jnp.where(low_first, other, own))
            xl, yx = divmod(p, 8)
            for core in range(2):
                for z in range(2):
                    m = xl * 128 + core * 64 + yx * 8 + pair * 2 + z
                    tiles[m] = both[core][z * 8:z * 8 + 8]
    for j in range(NBLK):
        for third in range(3):
            forcing_ref[third * 8:(third + 1) * 8, j * 128:(j + 1) * 128] = tiles[3 * j + third]
    for m in range(12):
        left[m * 8:(m + 1) * 8, :] = tiles[240 + m]
    for tap in range(9):
        for half in range(2):
            lanes = slice(half * 128, (half + 1) * 128)
            for g in range(8):
                conv_ref[tap, g * 8:(g + 1) * 8, lanes] = tiles[96 + (tap * 8 + g) * 2 + half]
            at = 5 * (2 * tap + half)
            conv_ref[tap, 64:CIN, lanes] = left[at:at + 5, :]


def unpack(core, own, other):
    return vmem_call(
        unpack_kernel,
        (
            jax.ShapeDtypeStruct((9, CIN, COUT), F32),
            jax.ShapeDtypeStruct((NCODE, WIDTH), F32),
        ),
        [pltpu.VMEM((96, 128), F32)],
        1000, 1000, core, own, other, smem=1,
    )


def per_device(
    fields, conv_weight, kernel_blocks, block_coords, forcing_table, forcing_codes, cotangent
):
    core = lax.axis_index("core")
    top = jnp.pad(fields[:, :, 7, :], ((0, 0), (0, PAD - CIN), (0, 0))).reshape(4 * PAD, 256)

    turned = kernel_blocks[0].T
    half = jnp.where(core == 0, turned[0:64], turned[64:128])
    marks = jnp.pad(block_coords.astype(BF16), ((0, 7), (0, 126)))
    payload = jnp.concatenate([half, marks], axis=0)
    payload, top = lax.optimization_barrier((payload, top))
    north = lax.ppermute(top, BAND, [(i, i + 1) for i in range(63)])
    column = lax.all_to_all(
        jnp.broadcast_to(payload[None], (8,) + payload.shape), "z", 0, 0, tiled=True
    )
    column, north = lax.optimization_barrier((column, north))
    own = lax.all_to_all(
        jnp.broadcast_to(column[None], (8,) + column.shape), ("y", "xh"), 0, 0, tiled=True
    ).reshape((NNZ,) + payload.shape)
    z, east = make_patches(fields.reshape(-1, 256), north)
    west = lax.ppermute(east, SECTION, [(i, (i + 1) % 4) for i in range(4)])
    latent = encode(z, conv_weight)
    own, latent = lax.optimization_barrier((own, latent))
    other = lax.ppermute(own, "core", [(0, 1), (1, 0)])
    coords = own[:, 64, 0:2].astype(jnp.int32)
    codes = forcing_codes.reshape(2, TOK)
    cot = cotangent.reshape(TOK, WIDTH)
    which = core.astype(jnp.int32).reshape(1)

    adjoint, partial = run_adjoint(coords, which, own, other, z, east, west, codes, cot)
    terms = lax.all_to_all(
        partial.reshape(32, 64, 128), ("xl", "core", "y", "xh"), 0, 0, tiled=True
    )
    state, keep, send = run_forward(
        coords, which, own, other, latent, east, west, conv_weight, forcing_table, codes,
        adjoint, cot,
    )
    terms, send = lax.optimization_barrier((terms, send))
    received = lax.ppermute(send, "core", [(0, 1), (1, 0)])
    latent_next = run_last(coords, which, own, other, state, forcing_table, codes)
    shared = jnp.sum(terms.astype(F32), axis=0).astype(BF16)
    spread = lax.all_to_all(
        jnp.broadcast_to(shared[None], (8, 64, 128)), "z", 0, 0, tiled=True
    )
    column = jnp.sum(spread.astype(F32), axis=0).astype(BF16)
    column, received, latent_next = lax.optimization_barrier((column, received, latent_next))
    chip = (keep + received.astype(F32)).astype(BF16).reshape(16, 256, 128)
    plane = lax.all_to_all(
        jnp.concatenate([chip, jnp.broadcast_to(column[None], (16, 64, 128))], axis=1),
        ("xl", "y", "xh"), 0, 0, tiled=True,
    )
    half_sums = plane[:, 256:320]
    other_sums = lax.ppermute(half_sums, "core", [(0, 1), (1, 0)])
    grad_conv, grad_forcing = unpack(which, half_sums, other_sums)
    quarter = jnp.sum(plane[:, 0:256].astype(F32), axis=0).astype(BF16).reshape(8, 32, 128)
    parts = lax.all_to_all(
        jnp.broadcast_to(quarter[None], (4, 8, 32, 128)).reshape(32, 32, 128),
        ("xl", "core", "z"), 0, 0, tiled=True,
    )
    quarters = jnp.sum(parts.reshape(2, 2, 8, 32, 128).astype(F32), axis=2)
    grad_blocks = jnp.transpose(quarters, (1, 0, 2, 3)).reshape(1, 128, 128)
    return (latent_next.reshape(cotangent.shape), grad_conv, grad_blocks, grad_forcing)


def solution(mesh):
    fine = Mesh(mesh.devices.reshape(2, 2, 4, 2, 8), ALL)
    return jax.shard_map(
        per_device,
        mesh=fine,
        in_specs=(
            P(None, None, BAND, SECTION),
            P(),
            P(BAND, None, None),
            P(BAND, None),
            P(),
            P(None, None, BAND, SECTION),
            P(None, BAND, SECTION, None),
        ),
        out_specs=(P(None, BAND, SECTION, None), P(), P(BAND, None, None), P()),
        check_vma=False,
    )
```

```python
import jax
import jax.numpy as jnp
from jax import lax
from jax.experimental import pallas as pl
from jax.experimental.pallas import tpu as pltpu
from jax.sharding import Mesh, PartitionSpec as P

BAND = ("y", "xh", "z")
SECTION = ("xl", "core")
ALL = ("xl", "core", "y", "xh", "z")
CIN, COUT, ROWS, PAD = 69, 256, 16, 80
TOK, WIDTH, NBLK, NNZ, NCODE = 128, 4096, 32, 64, 24
F32, BF16 = jnp.float32, jnp.bfloat16
VMEM_LIMIT = 56 * 1024 * 1024


def dot(a, b):
    return jnp.dot(a, b, preferred_element_type=F32)


def patches_kernel(fields_ref, north_ref, z_ref, east_ref, y0, y1, n0, n1):
    row = lax.broadcasted_iota(jnp.int32, (256, 256), 0)
    col = lax.broadcasted_iota(jnp.int32, (256, 256), 1)
    order = (row == (col & 7) * 32 + (col >> 3)).astype(BF16)

    def spread(step, carry):
        rows = pl.ds(pl.multiple_of(step * 368, 16), 368)
        mixed = dot(fields_ref[rows, :], order)
        y0[rows, :] = mixed[:, :128]
        y1[rows, :] = mixed[:, 128:]
        return carry

    lax.fori_loop(0, 6, spread, 0, unroll=3)
    y0[2208:2304, :] = jnp.zeros((96, 128), F32)
    y1[2208:2304, :] = jnp.zeros((96, 128), F32)
    mixed = dot(north_ref[...], order)
    n0[...] = mixed[:, :128]
    n1[...] = mixed[:, 128:]
    lane = lax.broadcasted_iota(jnp.int32, (16, 128), 1)

    def chunk(step, carry):
        for half, (rows_ref, top_ref) in enumerate(((y0, n0), (y1, n1))):
            for a in range(3):
                parts = []
                for s in range(4):
                    for r in range(4):
                        lat = 2 * r + a - 1
                        if lat < 0:
                            at = pl.ds(pl.multiple_of(s * PAD + step * 16, 16), 16)
                            parts.append(top_ref[at, :].astype(BF16))
                        else:
                            at = pl.ds(s * CIN * 8 + lat + step * 128, 16, stride=8)
                            parts.append(rows_ref[at, :].astype(BF16))
                for bit in (1, 2, 4, 8):
                    high = (lane & (8 * bit)) != 0
                    for i in range(16):
                        if i & bit:
                            continue
                        low_part, high_part = parts[i], parts[i | bit]
                        parts[i] = jnp.where(high, pltpu.roll(high_part, 8 * bit, 1), low_part)
                        parts[i | bit] = jnp.where(
                            high, high_part, pltpu.roll(low_part, 128 - 8 * bit, 1)
                        )
                for q in range(16):
                    at = pl.multiple_of((half * 16 + q + 1) * PAD + step * 16, 16)
                    z_ref[a, pl.ds(at, 16), :] = parts[q].astype(BF16)
                if half == 1:
                    at = pl.multiple_of(a * PAD + step * 16, 16)
                    east_ref[pl.ds(at, 16), :] = parts[15].astype(BF16)
        return carry

    lax.fori_loop(0, PAD // 16, chunk, 0)
    for a in range(3):
        z_ref[a, 0:PAD, :] = jnp.zeros((PAD, 128), BF16)


def make_patches(fields, north):
    return pl.pallas_call(
        patches_kernel,
        out_shape=(
            jax.ShapeDtypeStruct((3, 33 * PAD, 128), BF16),
            jax.ShapeDtypeStruct((3 * PAD, 128), BF16),
        ),
        in_specs=[pl.BlockSpec(memory_space=pltpu.VMEM)] * 2,
        out_specs=(pl.BlockSpec(memory_space=pltpu.VMEM),) * 2,
        scratch_shapes=[
            pltpu.VMEM((2304, 128), F32),
            pltpu.VMEM((2304, 128), F32),
            pltpu.VMEM((320, 128), F32),
            pltpu.VMEM((320, 128), F32),
        ],
        compiler_params=pltpu.CompilerParams(vmem_limit_bytes=VMEM_LIMIT),
        cost_estimate=pl.CostEstimate(flops=2 * 2528 * 256 * 256, bytes_accessed=4000000, transcendentals=0),
    )(fields, north)


OVER_ROWS = (((0,), (0,)), ((), ()))
OVER_LANES = (((1,), (1,)), ((), ()))


def rows_of(b):
    return pl.ds(pl.multiple_of(b * 128, 128), 128)


def vmem_call(kernel, out_shape, scratch, flops, size, *operands, smem=0):
    vmem = pl.BlockSpec(memory_space=pltpu.VMEM)
    scalar = pl.BlockSpec(memory_space=pltpu.SMEM)
    return pl.pallas_call(
        kernel,
        out_shape=out_shape,
        in_specs=[scalar] * smem + [vmem] * (len(operands) - smem),
        out_specs=tuple(vmem for _ in out_shape),
        scratch_shapes=scratch,
        compiler_params=pltpu.CompilerParams(vmem_limit_bytes=VMEM_LIMIT),
        cost_estimate=pl.CostEstimate(flops=flops, bytes_accessed=size, transcendentals=0),
    )(*operands)


def encode_kernel(z_ref, weight_ref, latent_ref, wt, wf):
    for a in range(3):
        wf[...] = jnp.zeros(wf.shape, F32)
        for b in range(3):
            wf[b * PAD:b * PAD + CIN, :] = weight_ref[3 * a + b].astype(F32)
        wt[a] = wf[...].T.astype(BF16)

    def encode_step(pair, carry):
        ks = [2 * pair, 2 * pair + 1]
        rows = [pl.ds(pl.multiple_of(k * 2 * PAD, 16), 3 * PAD) for k in ks]
        total = None
        for a in range(3):
            both = jnp.concatenate([z_ref[a, rows[0], :], z_ref[a, rows[1], :]], axis=1)
            term = dot(wt[a], both)
            total = term if a == 0 else total + term
        for u in range(2):
            latent_ref[pl.ds(ks[u], COUT, stride=16), :] = total[:, u * 128:(u + 1) * 128]
        return carry

    lax.fori_loop(0, 8, encode_step, 0, unroll=4)


def encode(z, weight):
    return vmem_call(
        encode_kernel,
        (jax.ShapeDtypeStruct((WIDTH, TOK), F32),),
        [pltpu.VMEM((3, COUT, 3 * PAD), BF16), pltpu.VMEM((3 * PAD, COUT), F32)],
        2 * 720 * 256 * 2048, 4 * 10**6, z, weight,
    )[0]


def first_column(east_ref, west_ref, a):
    lane = lax.broadcasted_iota(jnp.int32, (PAD, 128), 1)
    own = pltpu.roll(east_ref[a * PAD:(a + 1) * PAD, :].astype(F32), 1, 1)
    other = pltpu.roll(west_ref[a * PAD:(a + 1) * PAD, :].astype(F32), 128 - 7, 1)
    return jnp.where((lane & 7) == 0, other, own).astype(BF16)


def hot_codes(codes_ref, t):
    code = lax.broadcasted_iota(jnp.int32, (NCODE, TOK), 0)
    return (code == codes_ref[t:t + 1, :]).astype(BF16)


def block_of(n, low_first, own_ref, other_ref):
    own, other = own_ref[n, 0:64, :], other_ref[n, 0:64, :]
    return jnp.concatenate(
        [jnp.where(low_first, own, other), jnp.where(low_first, other, own)], axis=0
    )


def pull(coords_ref, low_first, own_ref, other_ref, source, target):
    def body(group, carry):
        items = []
        for u in range(UNROLL):
            n = group * UNROLL + u
            block = block_of(n, low_first, own_ref, other_ref)
            items.append((coords_ref[n, 0], dot(source(coords_ref[n, 1]), block)))
        for i, term in items:
            target[i] = target[i] + term
        return carry

    lax.fori_loop(0, NNZ // UNROLL, body, 0)


def push(coords_ref, low_first, own_ref, other_ref, source, target):
    def body(group, carry):
        items = []
        for u in range(UNROLL):
            n = group * UNROLL + u
            block = block_of(n, low_first, own_ref, other_ref)
            items.append((coords_ref[n, 1], dot(block, source(coords_ref[n, 0]))))
        for j, term in items:
            target[rows_of(j), :] = target[rows_of(j), :] + term
        return carry

    lax.fori_loop(0, NNZ // UNROLL, body, 0)


UNROLL = 64


def adjoint_kernel(
    coords_ref, core_ref, own_ref, other_ref, z_ref, east_ref, west_ref, codes_ref, cot_ref,
    adjoint_ref, out_ref,
    later, sums, turned, gc, left,
):
    low_first = core_ref[0] == 0
    for b in range(NBLK):
        cot = cot_ref[:, b * 128:(b + 1) * 128]
        later[b] = cot
        sums[b] = cot.astype(F32)
    pull(coords_ref, low_first, own_ref, other_ref, lambda j: later[j], sums)

    def between(b, carry):
        adjoint = sums[b].astype(BF16)
        adjoint_ref[b] = adjoint
        sums[b] = adjoint.astype(F32)
        return carry

    lax.fori_loop(0, NBLK, between, 0, unroll=4)
    pull(coords_ref, low_first, own_ref, other_ref, lambda j: adjoint_ref[j], sums)

    def end(b, carry):
        turned[rows_of(b), :] = sums[b].T
        return carry

    lax.fori_loop(0, NBLK, end, 0, unroll=4)
    hot = jnp.concatenate([hot_codes(codes_ref, 0), hot_codes(codes_ref, 1)], axis=1)
    for j in range(NBLK):
        both = jnp.concatenate([adjoint_ref[j], later[j]], axis=0)
        term = dot(hot, both).astype(BF16)
        for third in range(3):
            out_ref[3 * j + third] = term[third * 8:(third + 1) * 8, :]

    def conv_grads(pair, carry):
        adjoint, rows = [], []
        for u in range(2):
            k = 2 * pair + u
            adjoint.append(turned[pl.ds(k, COUT, stride=16), :].astype(BF16))
            rows.append(pl.ds(pl.multiple_of(k * 2 * PAD, 16), 3 * PAD))
        adjoint = jnp.concatenate(adjoint, axis=1)
        for a in range(3):
            patches = jnp.concatenate([z_ref[a, rows[0], :], z_ref[a, rows[1], :]], axis=1)
            gc[a] = gc[a] + lax.dot_general(
                patches, adjoint, OVER_LANES, preferred_element_type=F32
            )
        return carry

    gc[...] = jnp.zeros(gc.shape, F32)
    adjoint = turned[pl.ds(0, COUT, stride=16), :].astype(BF16)
    for a in range(3):
        gc[a, 0:PAD, :] = lax.dot_general(
            first_column(east_ref, west_ref, a), adjoint, OVER_LANES, preferred_element_type=F32
        )
    lax.fori_loop(0, 8, conv_grads, 0, unroll=4)
    left[...] = jnp.zeros(left.shape, F32)
    for tap in range(9):
        a, b = divmod(tap, 3)
        for half in range(2):
            lanes = slice(half * 128, (half + 1) * 128)
            for g in range(8):
                out_ref[96 + (tap * 8 + g) * 2 + half] = (
                    gc[a, b * PAD + g * 8:b * PAD + g * 8 + 8, lanes].astype(BF16)
                )
            at = 5 * (2 * tap + half)
            left[at:at + 5, :] = gc[a, b * PAD + 64:b * PAD + CIN, lanes]
    for m in range(16):
        out_ref[240 + m] = left[m * 8:(m + 1) * 8, :].astype(BF16)


def run_adjoint(coords, core, own, other, z, east, west, codes, cot):
    return vmem_call(
        adjoint_kernel,
        (
            jax.ShapeDtypeStruct((NBLK, TOK, 128), BF16),
            jax.ShapeDtypeStruct((256, 8, 128), BF16),
        ),
        [
            pltpu.VMEM((NBLK, TOK, 128), BF16),
            pltpu.VMEM((NBLK, TOK, 128), F32),
            pltpu.VMEM((WIDTH, TOK), F32),
            pltpu.VMEM((3, 3 * PAD, COUT), F32),
            pltpu.VMEM((128, 128), F32),
        ],
        1500 * 10**6, 8 * 10**6,
        coords, core, own, other, z, east, west, codes, cot, smem=2,
    )


def forward_kernel(
    coords_ref, core_ref, own_ref, other_ref, latent_ref, east_ref, west_ref, weight_ref,
    table_ref, codes_ref, adjoint_ref, cot_ref,
    state_ref, keep_ref, send_ref,
    sums, states, adjoints, wf,
):
    low_first = core_ref[0] == 0
    extra = jnp.zeros((COUT, TOK), F32)
    wf[...] = jnp.zeros(wf.shape, F32)
    for a in range(3):
        wf[0:CIN, :] = weight_ref[3 * a].astype(F32)
        extra += lax.dot_general(
            wf[...].astype(BF16), first_column(east_ref, west_ref, a), OVER_ROWS,
            preferred_element_type=F32,
        )
    at = pl.ds(0, COUT, stride=16)
    sums[...] = latent_ref[...]
    sums[at, :] = sums[at, :] + extra
    hot = hot_codes(codes_ref, 0)
    for b in range(NBLK):
        rows = slice(b * 128, (b + 1) * 128)
        state = sums[rows, :].astype(BF16)
        states[rows, 0:128] = state
        forcing = lax.dot_general(table_ref[:, rows], hot, OVER_ROWS, preferred_element_type=F32)
        sums[rows, :] = state.astype(F32) + forcing
        adjoints[b, 0:128, :] = adjoint_ref[b]
        adjoints[b, 128:256, :] = cot_ref[:, rows]
    push(
        coords_ref, low_first, own_ref, other_ref,
        lambda i: states[rows_of(i), 0:128], sums,
    )

    def end(b, carry):
        rows = rows_of(b)
        state = sums[rows, :].astype(BF16)
        states[rows, 128:256] = state
        state_ref[rows, :] = state
        return carry

    lax.fori_loop(0, NBLK, end, 0, unroll=4)

    def block_grads(group, carry):
        for u in range(UNROLL):
            n = group * UNROLL + u
            i, j = coords_ref[n, 0], coords_ref[n, 1]
            grad = dot(states[rows_of(i), :], adjoints[j])
            low, high = grad[0:64], grad[64:128]
            keep = jnp.where(low_first, low, high)
            send = jnp.where(low_first, high, low).astype(BF16)
            for x in range(2):
                keep_ref[x, n] = keep[x * 32:(x + 1) * 32]
                send_ref[x, n] = send[x * 32:(x + 1) * 32]
        return carry

    lax.fori_loop(0, NNZ // UNROLL, block_grads, 0)


def run_forward(coords, core, own, other, latent, east, west, weight, table, codes, adjoint, cot):
    return vmem_call(
        forward_kernel,
        (
            jax.ShapeDtypeStruct((WIDTH, TOK), BF16),
            jax.ShapeDtypeStruct((2, NNZ, 32, 128), F32),
            jax.ShapeDtypeStruct((2, NNZ, 32, 128), BF16),
        ),
        [
            pltpu.VMEM((WIDTH, TOK), F32),
            pltpu.VMEM((WIDTH, 2 * TOK), BF16),
            pltpu.VMEM((NBLK, 2 * TOK, 128), BF16),
            pltpu.VMEM((PAD, COUT), F32),
        ],
        1000, 1000,
        coords, core, own, other, latent, east, west, weight, table, codes, adjoint, cot, smem=2,
    )


def last_kernel(
    coords_ref, core_ref, own_ref, other_ref, state_ref, table_ref, codes_ref, next_ref, sums,
):
    low_first = core_ref[0] == 0
    hot = hot_codes(codes_ref, 1)
    for b in range(NBLK):
        rows = slice(b * 128, (b + 1) * 128)
        forcing = lax.dot_general(table_ref[:, rows], hot, OVER_ROWS, preferred_element_type=F32)
        sums[rows, :] = state_ref[rows, :].astype(F32) + forcing
    push(coords_ref, low_first, own_ref, other_ref, lambda i: state_ref[rows_of(i), :], sums)
    for b in range(NBLK):
        rows = slice(b * 128, (b + 1) * 128)
        next_ref[:, rows] = sums[rows, :].T.astype(BF16)


def run_last(coords, core, own, other, state, table, codes):
    return vmem_call(
        last_kernel,
        (jax.ShapeDtypeStruct((TOK, WIDTH), BF16),),
        [pltpu.VMEM((WIDTH, TOK), F32)],
        1000, 1000,
        coords, core, own, other, state, table, codes, smem=2,
    )[0]


def unpack_kernel(core_ref, own_ref, other_ref, conv_ref, forcing_ref, left):
    low_first = core_ref[0] == 0
    tiles = {}
    for p in range(16):
        for pair in range(4):
            own = own_ref[p, pair * 16:pair * 16 + 16, :].astype(F32)
            other = other_ref[p, pair * 16:pair * 16 + 16, :].astype(F32)
            both = (jnp.where(low_first, own, other), jnp.where(low_first, other, own))
            xl, yx = divmod(p, 8)
            for core in range(2):
                for z in range(2):
                    m = xl * 128 + core * 64 + yx * 8 + pair * 2 + z
                    tiles[m] = both[core][z * 8:z * 8 + 8]
    for j in range(NBLK):
        for third in range(3):
            forcing_ref[third * 8:(third + 1) * 8, j * 128:(j + 1) * 128] = tiles[3 * j + third]
    for m in range(12):
        left[m * 8:(m + 1) * 8, :] = tiles[240 + m]
    for tap in range(9):
        for half in range(2):
            lanes = slice(half * 128, (half + 1) * 128)
            for g in range(8):
                conv_ref[tap, g * 8:(g + 1) * 8, lanes] = tiles[96 + (tap * 8 + g) * 2 + half]
            at = 5 * (2 * tap + half)
            conv_ref[tap, 64:CIN, lanes] = left[at:at + 5, :]


def unpack(core, own, other):
    return vmem_call(
        unpack_kernel,
        (
            jax.ShapeDtypeStruct((9, CIN, COUT), F32),
            jax.ShapeDtypeStruct((NCODE, WIDTH), F32),
        ),
        [pltpu.VMEM((96, 128), F32)],
        1000, 1000, core, own, other, smem=1,
    )


def per_device(
    fields, conv_weight, kernel_blocks, block_coords, forcing_table, forcing_codes, cotangent
):
    core = lax.axis_index("core")
    top = jnp.pad(fields[:, :, 7, :], ((0, 0), (0, PAD - CIN), (0, 0))).reshape(4 * PAD, 256)

    turned = kernel_blocks[0].T
    half = jnp.where(core == 0, turned[0:64], turned[64:128])
    marks = jnp.pad(block_coords.astype(BF16), ((0, 7), (0, 126)))
    payload = jnp.concatenate([half, marks], axis=0)
    payload, top = lax.optimization_barrier((payload, top))
    north = lax.ppermute(top, BAND, [(i, i + 1) for i in range(63)])
    column = lax.all_to_all(
        jnp.broadcast_to(payload[None], (8,) + payload.shape), "z", 0, 0, tiled=True
    )
    column, north = lax.optimization_barrier((column, north))
    own = lax.all_to_all(
        jnp.broadcast_to(column[None], (8,) + column.shape), ("y", "xh"), 0, 0, tiled=True
    ).reshape((NNZ,) + payload.shape)
    z, east = make_patches(fields.reshape(-1, 256), north)
    west = lax.ppermute(east, SECTION, [(i, (i + 1) % 4) for i in range(4)])
    latent = encode(z, conv_weight)
    own, latent = lax.optimization_barrier((own, latent))
    other = lax.ppermute(own, "core", [(0, 1), (1, 0)])
    coords = own[:, 64, 0:2].astype(jnp.int32)
    codes = forcing_codes.reshape(2, TOK)
    cot = cotangent.reshape(TOK, WIDTH)
    which = core.astype(jnp.int32).reshape(1)

    adjoint, partial = run_adjoint(coords, which, own, other, z, east, west, codes, cot)
    terms = lax.all_to_all(
        partial.reshape(32, 64, 128), ("xl", "core", "y", "xh"), 0, 0, tiled=True
    )
    state, keep, send = run_forward(
        coords, which, own, other, latent, east, west, conv_weight, forcing_table, codes,
        adjoint, cot,
    )
    terms, send = lax.optimization_barrier((terms, send))
    received = lax.ppermute(send, "core", [(0, 1), (1, 0)])
    latent_next = run_last(coords, which, own, other, state, forcing_table, codes)
    shared = jnp.sum(terms.astype(F32), axis=0).astype(BF16)
    spread = lax.all_to_all(
        jnp.broadcast_to(shared[None], (8, 64, 128)), "z", 0, 0, tiled=True
    )
    chip = (keep + received.astype(F32)).astype(BF16).reshape(16, 256, 128)
    spread, chip = lax.optimization_barrier((spread, chip))
    column = jnp.sum(spread.astype(F32), axis=0).astype(BF16)
    plane = lax.all_to_all(
        jnp.concatenate([chip, jnp.broadcast_to(column[None], (16, 64, 128))], axis=1),
        ("xl", "y", "xh"), 0, 0, tiled=True,
    )
    plane, latent_next = lax.optimization_barrier((plane, latent_next))
    half_sums = plane[:, 256:320]
    other_sums = lax.ppermute(half_sums, "core", [(0, 1), (1, 0)])
    grad_conv, grad_forcing = unpack(which, half_sums, other_sums)
    quarter = jnp.sum(plane[:, 0:256].astype(F32), axis=0).astype(BF16).reshape(8, 32, 128)
    parts = lax.all_to_all(
        jnp.broadcast_to(quarter[None], (4, 8, 32, 128)).reshape(32, 32, 128),
        ("xl", "core", "z"), 0, 0, tiled=True,
    )
    quarters = jnp.sum(parts.reshape(2, 2, 8, 32, 128).astype(F32), axis=2)
    grad_blocks = jnp.transpose(quarters, (1, 0, 2, 3)).reshape(1, 128, 128)
    return (latent_next.reshape(cotangent.shape), grad_conv, grad_blocks, grad_forcing)


def solution(mesh):
    fine = Mesh(mesh.devices.reshape(2, 2, 4, 2, 8), ALL)
    return jax.shard_map(
        per_device,
        mesh=fine,
        in_specs=(
            P(None, None, BAND, SECTION),
            P(),
            P(BAND, None, None),
            P(BAND, None),
            P(),
            P(None, None, BAND, SECTION),
            P(None, BAND, SECTION, None),
        ),
        out_specs=(P(None, BAND, SECTION, None), P(), P(BAND, None, None), P()),
        check_vma=False,
    )
```

```python
import jax
import jax.numpy as jnp
from jax import lax
from jax.experimental import pallas as pl
from jax.experimental.pallas import tpu as pltpu
from jax.sharding import Mesh, PartitionSpec as P

BAND = ("y", "xh", "z")
SECTION = ("xl", "core")
ALL = ("xl", "core", "y", "xh", "z")
CIN, COUT, ROWS, PAD = 69, 256, 16, 80
TOK, WIDTH, NBLK, NNZ, NCODE = 128, 4096, 32, 64, 24
F32, BF16 = jnp.float32, jnp.bfloat16
VMEM_LIMIT = 56 * 1024 * 1024


def dot(a, b):
    return jnp.dot(a, b, preferred_element_type=F32)


def patches_kernel(fields_ref, north_ref, z_ref, east_ref, y0, y1, n0, n1):
    row = lax.broadcasted_iota(jnp.int32, (256, 256), 0)
    col = lax.broadcasted_iota(jnp.int32, (256, 256), 1)
    order = (row == (col & 7) * 32 + (col >> 3)).astype(BF16)

    def spread(step, carry):
        rows = pl.ds(pl.multiple_of(step * 368, 16), 368)
        mixed = dot(fields_ref[rows, :], order)
        y0[rows, :] = mixed[:, :128]
        y1[rows, :] = mixed[:, 128:]
        return carry

    lax.fori_loop(0, 6, spread, 0, unroll=3)
    y0[2208:2304, :] = jnp.zeros((96, 128), F32)
    y1[2208:2304, :] = jnp.zeros((96, 128), F32)
    mixed = dot(north_ref[...], order)
    n0[...] = mixed[:, :128]
    n1[...] = mixed[:, 128:]
    lane = lax.broadcasted_iota(jnp.int32, (16, 128), 1)

    def chunk(step, carry):
        for half, (rows_ref, top_ref) in enumerate(((y0, n0), (y1, n1))):
            for a in range(3):
                parts = []
                for s in range(4):
                    for r in range(4):
                        lat = 2 * r + a - 1
                        if lat < 0:
                            at = pl.ds(pl.multiple_of(s * PAD + step * 16, 16), 16)
                            parts.append(top_ref[at, :].astype(BF16))
                        else:
                            at = pl.ds(s * CIN * 8 + lat + step * 128, 16, stride=8)
                            parts.append(rows_ref[at, :].astype(BF16))
                for bit in (1, 2, 4, 8):
                    high = (lane & (8 * bit)) != 0
                    for i in range(16):
                        if i & bit:
                            continue
                        low_part, high_part = parts[i], parts[i | bit]
                        parts[i] = jnp.where(high, pltpu.roll(high_part, 8 * bit, 1), low_part)
                        parts[i | bit] = jnp.where(
                            high, high_part, pltpu.roll(low_part, 128 - 8 * bit, 1)
                        )
                for q in range(16):
                    at = pl.multiple_of((half * 16 + q + 1) * PAD + step * 16, 16)
                    z_ref[a, pl.ds(at, 16), :] = parts[q].astype(BF16)
                if half == 1:
                    at = pl.multiple_of(a * PAD + step * 16, 16)
                    east_ref[pl.ds(at, 16), :] = parts[15].astype(BF16)
        return carry

    lax.fori_loop(0, PAD // 16, chunk, 0)
    for a in range(3):
        z_ref[a, 0:PAD, :] = jnp.zeros((PAD, 128), BF16)


def make_patches(fields, north):
    return pl.pallas_call(
        patches_kernel,
        out_shape=(
            jax.ShapeDtypeStruct((3, 33 * PAD, 128), BF16),
            jax.ShapeDtypeStruct((3 * PAD, 128), BF16),
        ),
        in_specs=[pl.BlockSpec(memory_space=pltpu.VMEM)] * 2,
        out_specs=(pl.BlockSpec(memory_space=pltpu.VMEM),) * 2,
        scratch_shapes=[
            pltpu.VMEM((2304, 128), F32),
            pltpu.VMEM((2304, 128), F32),
            pltpu.VMEM((320, 128), F32),
            pltpu.VMEM((320, 128), F32),
        ],
        compiler_params=pltpu.CompilerParams(vmem_limit_bytes=VMEM_LIMIT),
        cost_estimate=pl.CostEstimate(flops=2 * 2528 * 256 * 256, bytes_accessed=4000000, transcendentals=0),
    )(fields, north)


OVER_ROWS = (((0,), (0,)), ((), ()))
OVER_LANES = (((1,), (1,)), ((), ()))


def rows_of(b):
    return pl.ds(pl.multiple_of(b * 128, 128), 128)


def vmem_call(kernel, out_shape, scratch, flops, size, *operands, smem=0):
    vmem = pl.BlockSpec(memory_space=pltpu.VMEM)
    scalar = pl.BlockSpec(memory_space=pltpu.SMEM)
    return pl.pallas_call(
        kernel,
        out_shape=out_shape,
        in_specs=[scalar] * smem + [vmem] * (len(operands) - smem),
        out_specs=tuple(vmem for _ in out_shape),
        scratch_shapes=scratch,
        compiler_params=pltpu.CompilerParams(vmem_limit_bytes=VMEM_LIMIT),
        cost_estimate=pl.CostEstimate(flops=flops, bytes_accessed=size, transcendentals=0),
    )(*operands)


def prepare_kernel(coords_ref, core_ref, block_ref, copies_ref):
    turned = block_ref[0].astype(F32).T
    half = jnp.where(core_ref[0] == 0, turned[0:64], turned[64:128])
    row = lax.broadcasted_iota(jnp.int32, (8, 128), 0)
    lane = lax.broadcasted_iota(jnp.int32, (8, 128), 1)
    mark = jnp.where(lane == 0, coords_ref[0, 0], jnp.where(lane == 1, coords_ref[0, 1], 0))
    mark = jnp.where(row == 0, mark, 0).astype(F32)
    payload = jnp.concatenate([half, mark], axis=0).astype(BF16)
    for z in range(8):
        copies_ref[z] = payload


def prepare(coords, core, block):
    return vmem_call(
        prepare_kernel, (jax.ShapeDtypeStruct((8, 72, 128), BF16),), [], 1000, 1000,
        coords, core, block, smem=2,
    )[0]


def encode_kernel(z_ref, weight_ref, latent_ref, wt, wf):
    for a in range(3):
        wf[...] = jnp.zeros(wf.shape, F32)
        for b in range(3):
            wf[b * PAD:b * PAD + CIN, :] = weight_ref[3 * a + b].astype(F32)
        wt[a] = wf[...].T.astype(BF16)

    def encode_step(pair, carry):
        ks = [2 * pair, 2 * pair + 1]
        rows = [pl.ds(pl.multiple_of(k * 2 * PAD, 16), 3 * PAD) for k in ks]
        total = None
        for a in range(3):
            both = jnp.concatenate([z_ref[a, rows[0], :], z_ref[a, rows[1], :]], axis=1)
            term = dot(wt[a], both)
            total = term if a == 0 else total + term
        for u in range(2):
            latent_ref[pl.ds(ks[u], COUT, stride=16), :] = total[:, u * 128:(u + 1) * 128]
        return carry

    lax.fori_loop(0, 8, encode_step, 0, unroll=4)


def encode(z, weight):
    return vmem_call(
        encode_kernel,
        (jax.ShapeDtypeStruct((WIDTH, TOK), F32),),
        [pltpu.VMEM((3, COUT, 3 * PAD), BF16), pltpu.VMEM((3 * PAD, COUT), F32)],
        2 * 720 * 256 * 2048, 4 * 10**6, z, weight,
    )[0]


def first_column(east_ref, west_ref, a):
    lane = lax.broadcasted_iota(jnp.int32, (PAD, 128), 1)
    own = pltpu.roll(east_ref[a * PAD:(a + 1) * PAD, :].astype(F32), 1, 1)
    other = pltpu.roll(west_ref[a * PAD:(a + 1) * PAD, :].astype(F32), 128 - 7, 1)
    return jnp.where((lane & 7) == 0, other, own).astype(BF16)


def hot_codes(codes_ref, t):
    code = lax.broadcasted_iota(jnp.int32, (NCODE, TOK), 0)
    return (code == codes_ref[t:t + 1, :]).astype(BF16)


def block_of(n, low_first, own_ref, other_ref):
    own, other = own_ref[n, 0:64, :], other_ref[n, 0:64, :]
    return jnp.concatenate(
        [jnp.where(low_first, own, other), jnp.where(low_first, other, own)], axis=0
    )


def pull(coords_ref, low_first, own_ref, other_ref, source, target):
    def body(group, carry):
        items = []
        for u in range(UNROLL):
            n = group * UNROLL + u
            block = block_of(n, low_first, own_ref, other_ref)
            items.append((coords_ref[n, 0], dot(source(coords_ref[n, 1]), block)))
        for i, term in items:
            target[i] = target[i] + term
        return carry

    lax.fori_loop(0, NNZ // UNROLL, body, 0)


def push(coords_ref, low_first, own_ref, other_ref, source, target):
    def body(group, carry):
        items = []
        for u in range(UNROLL):
            n = group * UNROLL + u
            block = block_of(n, low_first, own_ref, other_ref)
            items.append((coords_ref[n, 1], dot(block, source(coords_ref[n, 0]))))
        for j, term in items:
            target[rows_of(j), :] = target[rows_of(j), :] + term
        return carry

    lax.fori_loop(0, NNZ // UNROLL, body, 0)


UNROLL = 64


def adjoint_kernel(
    coords_ref, core_ref, own_ref, other_ref, z_ref, east_ref, west_ref, codes_ref, cot_ref,
    adjoint_ref, out_ref,
    later, sums, turned, gc, left,
):
    low_first = core_ref[0] == 0
    for b in range(NBLK):
        cot = cot_ref[:, b * 128:(b + 1) * 128]
        later[b] = cot
        sums[b] = cot.astype(F32)
    pull(coords_ref, low_first, own_ref, other_ref, lambda j: later[j], sums)

    def between(b, carry):
        adjoint = sums[b].astype(BF16)
        adjoint_ref[b] = adjoint
        sums[b] = adjoint.astype(F32)
        return carry

    lax.fori_loop(0, NBLK, between, 0, unroll=4)
    pull(coords_ref, low_first, own_ref, other_ref, lambda j: adjoint_ref[j], sums)

    def end(b, carry):
        turned[rows_of(b), :] = sums[b].T
        return carry

    lax.fori_loop(0, NBLK, end, 0, unroll=4)
    hot = jnp.concatenate([hot_codes(codes_ref, 0), hot_codes(codes_ref, 1)], axis=1)
    for j in range(NBLK):
        both = jnp.concatenate([adjoint_ref[j], later[j]], axis=0)
        term = dot(hot, both).astype(BF16)
        for third in range(3):
            out_ref[3 * j + third] = term[third * 8:(third + 1) * 8, :]

    def conv_grads(pair, carry):
        adjoint, rows = [], []
        for u in range(2):
            k = 2 * pair + u
            adjoint.append(turned[pl.ds(k, COUT, stride=16), :].astype(BF16))
            rows.append(pl.ds(pl.multiple_of(k * 2 * PAD, 16), 3 * PAD))
        adjoint = jnp.concatenate(adjoint, axis=1)
        for a in range(3):
            patches = jnp.concatenate([z_ref[a, rows[0], :], z_ref[a, rows[1], :]], axis=1)
            gc[a] = gc[a] + lax.dot_general(
                patches, adjoint, OVER_LANES, preferred_element_type=F32
            )
        return carry

    gc[...] = jnp.zeros(gc.shape, F32)
    adjoint = turned[pl.ds(0, COUT, stride=16), :].astype(BF16)
    for a in range(3):
        gc[a, 0:PAD, :] = lax.dot_general(
            first_column(east_ref, west_ref, a), adjoint, OVER_LANES, preferred_element_type=F32
        )
    lax.fori_loop(0, 8, conv_grads, 0, unroll=4)
    left[...] = jnp.zeros(left.shape, F32)
    for tap in range(9):
        a, b = divmod(tap, 3)
        for half in range(2):
            lanes = slice(half * 128, (half + 1) * 128)
            for g in range(8):
                out_ref[96 + (tap * 8 + g) * 2 + half] = (
                    gc[a, b * PAD + g * 8:b * PAD + g * 8 + 8, lanes].astype(BF16)
                )
            at = 5 * (2 * tap + half)
            left[at:at + 5, :] = gc[a, b * PAD + 64:b * PAD + CIN, lanes]
    for m in range(16):
        out_ref[240 + m] = left[m * 8:(m + 1) * 8, :].astype(BF16)


def run_adjoint(coords, core, own, other, z, east, west, codes, cot):
    return vmem_call(
        adjoint_kernel,
        (
            jax.ShapeDtypeStruct((NBLK, TOK, 128), BF16),
            jax.ShapeDtypeStruct((256, 8, 128), BF16),
        ),
        [
            pltpu.VMEM((NBLK, TOK, 128), BF16),
            pltpu.VMEM((NBLK, TOK, 128), F32),
            pltpu.VMEM((WIDTH, TOK), F32),
            pltpu.VMEM((3, 3 * PAD, COUT), F32),
            pltpu.VMEM((128, 128), F32),
        ],
        1500 * 10**6, 8 * 10**6,
        coords, core, own, other, z, east, west, codes, cot, smem=2,
    )


def forward_kernel(
    coords_ref, core_ref, own_ref, other_ref, latent_ref, east_ref, west_ref, weight_ref,
    table_ref, codes_ref, adjoint_ref, cot_ref,
    state_ref, keep_ref, send_ref,
    sums, states, adjoints, wf,
):
    low_first = core_ref[0] == 0
    extra = jnp.zeros((COUT, TOK), F32)
    wf[...] = jnp.zeros(wf.shape, F32)
    for a in range(3):
        wf[0:CIN, :] = weight_ref[3 * a].astype(F32)
        extra += lax.dot_general(
            wf[...].astype(BF16), first_column(east_ref, west_ref, a), OVER_ROWS,
            preferred_element_type=F32,
        )
    at = pl.ds(0, COUT, stride=16)
    sums[...] = latent_ref[...]
    sums[at, :] = sums[at, :] + extra
    hot = hot_codes(codes_ref, 0)
    for b in range(NBLK):
        rows = slice(b * 128, (b + 1) * 128)
        state = sums[rows, :].astype(BF16)
        states[rows, 0:128] = state
        forcing = lax.dot_general(table_ref[:, rows], hot, OVER_ROWS, preferred_element_type=F32)
        sums[rows, :] = state.astype(F32) + forcing
        adjoints[b, 0:128, :] = adjoint_ref[b]
        adjoints[b, 128:256, :] = cot_ref[:, rows]
    push(
        coords_ref, low_first, own_ref, other_ref,
        lambda i: states[rows_of(i), 0:128], sums,
    )

    def end(b, carry):
        rows = rows_of(b)
        state = sums[rows, :].astype(BF16)
        states[rows, 128:256] = state
        state_ref[rows, :] = state
        return carry

    lax.fori_loop(0, NBLK, end, 0, unroll=4)

    def block_grads(group, carry):
        for u in range(UNROLL):
            n = group * UNROLL + u
            i, j = coords_ref[n, 0], coords_ref[n, 1]
            grad = dot(states[rows_of(i), :], adjoints[j])
            low, high = grad[0:64], grad[64:128]
            keep = jnp.where(low_first, low, high)
            send = jnp.where(low_first, high, low).astype(BF16)
            for x in range(2):
                keep_ref[x, n] = keep[x * 32:(x + 1) * 32]
                send_ref[x, n] = send[x * 32:(x + 1) * 32]
        return carry

    lax.fori_loop(0, NNZ // UNROLL, block_grads, 0)


def run_forward(coords, core, own, other, latent, east, west, weight, table, codes, adjoint, cot):
    return vmem_call(
        forward_kernel,
        (
            jax.ShapeDtypeStruct((WIDTH, TOK), BF16),
            jax.ShapeDtypeStruct((2, NNZ, 32, 128), F32),
            jax.ShapeDtypeStruct((2, NNZ, 32, 128), BF16),
        ),
        [
            pltpu.VMEM((WIDTH, TOK), F32),
            pltpu.VMEM((WIDTH, 2 * TOK), BF16),
            pltpu.VMEM((NBLK, 2 * TOK, 128), BF16),
            pltpu.VMEM((PAD, COUT), F32),
        ],
        1000, 1000,
        coords, core, own, other, latent, east, west, weight, table, codes, adjoint, cot, smem=2,
    )


def last_kernel(
    coords_ref, core_ref, own_ref, other_ref, state_ref, table_ref, codes_ref, next_ref, sums,
):
    low_first = core_ref[0] == 0
    hot = hot_codes(codes_ref, 1)
    for b in range(NBLK):
        rows = slice(b * 128, (b + 1) * 128)
        forcing = lax.dot_general(table_ref[:, rows], hot, OVER_ROWS, preferred_element_type=F32)
        sums[rows, :] = state_ref[rows, :].astype(F32) + forcing
    push(coords_ref, low_first, own_ref, other_ref, lambda i: state_ref[rows_of(i), :], sums)
    for b in range(NBLK):
        rows = slice(b * 128, (b + 1) * 128)
        next_ref[:, rows] = sums[rows, :].T.astype(BF16)


def run_last(coords, core, own, other, state, table, codes):
    return vmem_call(
        last_kernel,
        (jax.ShapeDtypeStruct((TOK, WIDTH), BF16),),
        [pltpu.VMEM((WIDTH, TOK), F32)],
        1000, 1000,
        coords, core, own, other, state, table, codes, smem=2,
    )[0]


def unpack_kernel(core_ref, own_ref, other_ref, conv_ref, forcing_ref, left):
    low_first = core_ref[0] == 0
    tiles = {}
    for p in range(16):
        for pair in range(4):
            own = own_ref[p, pair * 16:pair * 16 + 16, :].astype(F32)
            other = other_ref[p, pair * 16:pair * 16 + 16, :].astype(F32)
            both = (jnp.where(low_first, own, other), jnp.where(low_first, other, own))
            xl, yx = divmod(p, 8)
            for core in range(2):
                for z in range(2):
                    m = xl * 128 + core * 64 + yx * 8 + pair * 2 + z
                    tiles[m] = both[core][z * 8:z * 8 + 8]
    for j in range(NBLK):
        for third in range(3):
            forcing_ref[third * 8:(third + 1) * 8, j * 128:(j + 1) * 128] = tiles[3 * j + third]
    for m in range(12):
        left[m * 8:(m + 1) * 8, :] = tiles[240 + m]
    for tap in range(9):
        for half in range(2):
            lanes = slice(half * 128, (half + 1) * 128)
            for g in range(8):
                conv_ref[tap, g * 8:(g + 1) * 8, lanes] = tiles[96 + (tap * 8 + g) * 2 + half]
            at = 5 * (2 * tap + half)
            conv_ref[tap, 64:CIN, lanes] = left[at:at + 5, :]


def unpack(core, own, other):
    return vmem_call(
        unpack_kernel,
        (
            jax.ShapeDtypeStruct((9, CIN, COUT), F32),
            jax.ShapeDtypeStruct((NCODE, WIDTH), F32),
        ),
        [pltpu.VMEM((96, 128), F32)],
        1000, 1000, core, own, other, smem=1,
    )


def per_device(
    fields, conv_weight, kernel_blocks, block_coords, forcing_table, forcing_codes, cotangent
):
    core = lax.axis_index("core")
    top = jnp.pad(fields[:, :, 7, :], ((0, 0), (0, PAD - CIN), (0, 0))).reshape(4 * PAD, 256)

    which = core.astype(jnp.int32).reshape(1)
    copies = prepare(block_coords, which, kernel_blocks)
    copies, top = lax.optimization_barrier((copies, top))
    north = lax.ppermute(top, BAND, [(i, i + 1) for i in range(63)])
    column = lax.all_to_all(copies, "z", 0, 0, tiled=True)
    column, north = lax.optimization_barrier((column, north))
    own = lax.all_to_all(
        jnp.broadcast_to(column[None], (8,) + column.shape), ("y", "xh"), 0, 0, tiled=True
    ).reshape(NNZ, 72, 128)
    z, east = make_patches(fields.reshape(-1, 256), north)
    west = lax.ppermute(east, SECTION, [(i, (i + 1) % 4) for i in range(4)])
    latent = encode(z, conv_weight)
    own, latent = lax.optimization_barrier((own, latent))
    other = lax.ppermute(own, "core", [(0, 1), (1, 0)])
    coords = own[:, 64, 0:2].astype(jnp.int32)
    codes = forcing_codes.reshape(2, TOK)
    cot = cotangent.reshape(TOK, WIDTH)

    adjoint, partial = run_adjoint(coords, which, own, other, z, east, west, codes, cot)
    terms = lax.all_to_all(
        partial.reshape(32, 64, 128), ("xl", "core", "y", "xh"), 0, 0, tiled=True
    )
    state, keep, send = run_forward(
        coords, which, own, other, latent, east, west, conv_weight, forcing_table, codes,
        adjoint, cot,
    )
    terms, send = lax.optimization_barrier((terms, send))
    received = lax.ppermute(send, "core", [(0, 1), (1, 0)])
    latent_next = run_last(coords, which, own, other, state, forcing_table, codes)
    shared = jnp.sum(terms.astype(F32), axis=0).astype(BF16)
    spread = lax.all_to_all(
        jnp.broadcast_to(shared[None], (8, 64, 128)), "z", 0, 0, tiled=True
    )
    chip = (keep + received.astype(F32)).astype(BF16).reshape(16, 256, 128)
    spread, chip = lax.optimization_barrier((spread, chip))
    column = jnp.sum(spread.astype(F32), axis=0).astype(BF16)
    plane = lax.all_to_all(
        jnp.concatenate([chip, jnp.broadcast_to(column[None], (16, 64, 128))], axis=1),
        ("xl", "y", "xh"), 0, 0, tiled=True,
    )
    plane, latent_next = lax.optimization_barrier((plane, latent_next))
    half_sums = plane[:, 256:320]
    other_sums = lax.ppermute(half_sums, "core", [(0, 1), (1, 0)])
    grad_conv, grad_forcing = unpack(which, half_sums, other_sums)
    quarter = jnp.sum(plane[:, 0:256].astype(F32), axis=0).astype(BF16).reshape(8, 32, 128)
    parts = lax.all_to_all(
        jnp.broadcast_to(quarter[None], (4, 8, 32, 128)).reshape(32, 32, 128),
        ("xl", "core", "z"), 0, 0, tiled=True,
    )
    quarters = jnp.sum(parts.reshape(2, 2, 8, 32, 128).astype(F32), axis=2)
    grad_blocks = jnp.transpose(quarters, (1, 0, 2, 3)).reshape(1, 128, 128)
    return (latent_next.reshape(cotangent.shape), grad_conv, grad_blocks, grad_forcing)


def solution(mesh):
    fine = Mesh(mesh.devices.reshape(2, 2, 4, 2, 8), ALL)
    return jax.shard_map(
        per_device,
        mesh=fine,
        in_specs=(
            P(None, None, BAND, SECTION),
            P(),
            P(BAND, None, None),
            P(BAND, None),
            P(),
            P(None, None, BAND, SECTION),
            P(None, BAND, SECTION, None),
        ),
        out_specs=(P(None, BAND, SECTION, None), P(), P(BAND, None, None), P()),
        check_vma=False,
    )
```

```python
import jax
import jax.numpy as jnp
from jax import lax
from jax.experimental import pallas as pl
from jax.experimental.pallas import tpu as pltpu
from jax.sharding import Mesh, PartitionSpec as P

BAND = ("y", "xh", "z")
SECTION = ("xl", "core")
ALL = ("xl", "core", "y", "xh", "z")
CIN, COUT, ROWS, PAD = 69, 256, 16, 80
TOK, WIDTH, NBLK, NNZ, NCODE = 128, 4096, 32, 64, 24
F32, BF16 = jnp.float32, jnp.bfloat16
VMEM_LIMIT = 56 * 1024 * 1024


def dot(a, b):
    return jnp.dot(a, b, preferred_element_type=F32)


def patches_kernel(fields_ref, north_ref, z_ref, east_ref, y0, y1, n0, n1):
    row = lax.broadcasted_iota(jnp.int32, (256, 256), 0)
    col = lax.broadcasted_iota(jnp.int32, (256, 256), 1)
    order = (row == (col & 7) * 32 + (col >> 3)).astype(BF16)

    def spread(step, carry):
        rows = pl.ds(pl.multiple_of(step * 368, 16), 368)
        mixed = dot(fields_ref[rows, :], order)
        y0[rows, :] = mixed[:, :128]
        y1[rows, :] = mixed[:, 128:]
        return carry

    lax.fori_loop(0, 6, spread, 0, unroll=3)
    y0[2208:2304, :] = jnp.zeros((96, 128), F32)
    y1[2208:2304, :] = jnp.zeros((96, 128), F32)
    mixed = dot(north_ref[...], order)
    n0[...] = mixed[:, :128]
    n1[...] = mixed[:, 128:]
    lane = lax.broadcasted_iota(jnp.int32, (16, 128), 1)

    def chunk(step, carry):
        for half, (rows_ref, top_ref) in enumerate(((y0, n0), (y1, n1))):
            for a in range(3):
                parts = []
                for s in range(4):
                    for r in range(4):
                        lat = 2 * r + a - 1
                        if lat < 0:
                            at = pl.ds(pl.multiple_of(s * PAD + step * 16, 16), 16)
                            parts.append(top_ref[at, :].astype(BF16))
                        else:
                            at = pl.ds(s * CIN * 8 + lat + step * 128, 16, stride=8)
                            parts.append(rows_ref[at, :].astype(BF16))
                for bit in (1, 2, 4, 8):
                    high = (lane & (8 * bit)) != 0
                    for i in range(16):
                        if i & bit:
                            continue
                        low_part, high_part = parts[i], parts[i | bit]
                        parts[i] = jnp.where(high, pltpu.roll(high_part, 8 * bit, 1), low_part)
                        parts[i | bit] = jnp.where(
                            high, high_part, pltpu.roll(low_part, 128 - 8 * bit, 1)
                        )
                for q in range(16):
                    at = pl.multiple_of((half * 16 + q + 1) * PAD + step * 16, 16)
                    z_ref[a, pl.ds(at, 16), :] = parts[q].astype(BF16)
                if half == 1:
                    at = pl.multiple_of(a * PAD + step * 16, 16)
                    east_ref[pl.ds(at, 16), :] = parts[15].astype(BF16)
        return carry

    lax.fori_loop(0, PAD // 16, chunk, 0)
    for a in range(3):
        z_ref[a, 0:PAD, :] = jnp.zeros((PAD, 128), BF16)


def make_patches(fields, north):
    return pl.pallas_call(
        patches_kernel,
        out_shape=(
            jax.ShapeDtypeStruct((3, 33 * PAD, 128), BF16),
            jax.ShapeDtypeStruct((3 * PAD, 128), BF16),
        ),
        in_specs=[pl.BlockSpec(memory_space=pltpu.VMEM)] * 2,
        out_specs=(pl.BlockSpec(memory_space=pltpu.VMEM),) * 2,
        scratch_shapes=[
            pltpu.VMEM((2304, 128), F32),
            pltpu.VMEM((2304, 128), F32),
            pltpu.VMEM((320, 128), F32),
            pltpu.VMEM((320, 128), F32),
        ],
        compiler_params=pltpu.CompilerParams(vmem_limit_bytes=VMEM_LIMIT),
        cost_estimate=pl.CostEstimate(flops=2 * 2528 * 256 * 256, bytes_accessed=4000000, transcendentals=0),
    )(fields, north)


OVER_ROWS = (((0,), (0,)), ((), ()))
OVER_LANES = (((1,), (1,)), ((), ()))


def rows_of(b):
    return pl.ds(pl.multiple_of(b * 128, 128), 128)


def vmem_call(kernel, out_shape, scratch, flops, size, *operands, smem=0, hbm=()):
    vmem = pl.BlockSpec(memory_space=pltpu.VMEM)
    scalar = pl.BlockSpec(memory_space=pltpu.SMEM)
    return pl.pallas_call(
        kernel,
        out_shape=out_shape,
        in_specs=[
            scalar if i < smem else pl.BlockSpec(memory_space=pl.ANY) if i in hbm else vmem
            for i in range(len(operands))
        ],
        out_specs=tuple(vmem for _ in out_shape),
        scratch_shapes=scratch,
        compiler_params=pltpu.CompilerParams(vmem_limit_bytes=VMEM_LIMIT),
        cost_estimate=pl.CostEstimate(flops=flops, bytes_accessed=size, transcendentals=0),
    )(*operands)


def prepare_kernel(coords_ref, core_ref, block_ref, copies_ref):
    turned = block_ref[0].astype(F32).T
    half = jnp.where(core_ref[0] == 0, turned[0:64], turned[64:128])
    row = lax.broadcasted_iota(jnp.int32, (8, 128), 0)
    lane = lax.broadcasted_iota(jnp.int32, (8, 128), 1)
    mark = jnp.where(lane == 0, coords_ref[0, 0], jnp.where(lane == 1, coords_ref[0, 1], 0))
    mark = jnp.where(row == 0, mark, 0).astype(F32)
    payload = jnp.concatenate([half, mark], axis=0).astype(BF16)
    for z in range(8):
        copies_ref[z] = payload


def prepare(coords, core, block):
    return vmem_call(
        prepare_kernel, (jax.ShapeDtypeStruct((8, 72, 128), BF16),), [], 1000, 1000,
        coords, core, block, smem=2,
    )[0]


def encode_kernel(z_ref, weight_ref, latent_ref, wt, wf):
    for a in range(3):
        wf[...] = jnp.zeros(wf.shape, F32)
        for b in range(3):
            wf[b * PAD:b * PAD + CIN, :] = weight_ref[3 * a + b].astype(F32)
        wt[a] = wf[...].T.astype(BF16)

    def encode_step(pair, carry):
        ks = [2 * pair, 2 * pair + 1]
        rows = [pl.ds(pl.multiple_of(k * 2 * PAD, 16), 3 * PAD) for k in ks]
        total = None
        for a in range(3):
            both = jnp.concatenate([z_ref[a, rows[0], :], z_ref[a, rows[1], :]], axis=1)
            term = dot(wt[a], both)
            total = term if a == 0 else total + term
        for u in range(2):
            latent_ref[pl.ds(ks[u], COUT, stride=16), :] = total[:, u * 128:(u + 1) * 128]
        return carry

    lax.fori_loop(0, 8, encode_step, 0, unroll=4)


def encode(z, weight):
    return vmem_call(
        encode_kernel,
        (jax.ShapeDtypeStruct((WIDTH, TOK), F32),),
        [pltpu.VMEM((3, COUT, 3 * PAD), BF16), pltpu.VMEM((3 * PAD, COUT), F32)],
        2 * 720 * 256 * 2048, 4 * 10**6, z, weight,
    )[0]


def first_column(east_ref, west_ref, a):
    lane = lax.broadcasted_iota(jnp.int32, (PAD, 128), 1)
    own = pltpu.roll(east_ref[a * PAD:(a + 1) * PAD, :].astype(F32), 1, 1)
    other = pltpu.roll(west_ref[a * PAD:(a + 1) * PAD, :].astype(F32), 128 - 7, 1)
    return jnp.where((lane & 7) == 0, other, own).astype(BF16)


def hot_codes(codes_ref, t):
    code = lax.broadcasted_iota(jnp.int32, (NCODE, TOK), 0)
    return (code == codes_ref[t:t + 1, :]).astype(BF16)


def block_of(n, low_first, own_ref, other_ref):
    own, other = own_ref[n, 0:64, :], other_ref[n, 0:64, :]
    return jnp.concatenate(
        [jnp.where(low_first, own, other), jnp.where(low_first, other, own)], axis=0
    )


def pull(coords_ref, low_first, own_ref, other_ref, source, target):
    def body(group, carry):
        items = []
        for u in range(UNROLL):
            n = group * UNROLL + u
            block = block_of(n, low_first, own_ref, other_ref)
            items.append((coords_ref[n, 0], dot(source(coords_ref[n, 1]), block)))
        for i, term in items:
            target[i] = target[i] + term
        return carry

    lax.fori_loop(0, NNZ // UNROLL, body, 0)


def push(coords_ref, low_first, own_ref, other_ref, source, target):
    def body(group, carry):
        items = []
        for u in range(UNROLL):
            n = group * UNROLL + u
            block = block_of(n, low_first, own_ref, other_ref)
            items.append((coords_ref[n, 1], dot(block, source(coords_ref[n, 0]))))
        for j, term in items:
            target[rows_of(j), :] = target[rows_of(j), :] + term
        return carry

    lax.fori_loop(0, NNZ // UNROLL, body, 0)


UNROLL = 64


def adjoint_kernel(
    coords_ref, core_ref, own_ref, other_ref, z_hbm, east_ref, west_ref, codes_ref, cot_ref,
    adjoint_ref, out_ref,
    later, sums, turned, gc, left, z_ref, z_sem,
):
    z_copy = pltpu.make_async_copy(z_hbm, z_ref, z_sem)
    z_copy.start()
    low_first = core_ref[0] == 0
    for b in range(NBLK):
        cot = cot_ref[:, b * 128:(b + 1) * 128]
        later[b] = cot
        sums[b] = cot.astype(F32)
    pull(coords_ref, low_first, own_ref, other_ref, lambda j: later[j], sums)

    def between(b, carry):
        adjoint = sums[b].astype(BF16)
        adjoint_ref[b] = adjoint
        sums[b] = adjoint.astype(F32)
        return carry

    lax.fori_loop(0, NBLK, between, 0, unroll=4)
    pull(coords_ref, low_first, own_ref, other_ref, lambda j: adjoint_ref[j], sums)

    def end(b, carry):
        turned[rows_of(b), :] = sums[b].T
        return carry

    lax.fori_loop(0, NBLK, end, 0, unroll=4)
    hot = jnp.concatenate([hot_codes(codes_ref, 0), hot_codes(codes_ref, 1)], axis=1)
    for j in range(NBLK):
        both = jnp.concatenate([adjoint_ref[j], later[j]], axis=0)
        term = dot(hot, both).astype(BF16)
        for third in range(3):
            out_ref[3 * j + third] = term[third * 8:(third + 1) * 8, :]

    def conv_grads(pair, carry):
        adjoint, rows = [], []
        for u in range(2):
            k = 2 * pair + u
            adjoint.append(turned[pl.ds(k, COUT, stride=16), :].astype(BF16))
            rows.append(pl.ds(pl.multiple_of(k * 2 * PAD, 16), 3 * PAD))
        adjoint = jnp.concatenate(adjoint, axis=1)
        for a in range(3):
            patches = jnp.concatenate([z_ref[a, rows[0], :], z_ref[a, rows[1], :]], axis=1)
            gc[a] = gc[a] + lax.dot_general(
                patches, adjoint, OVER_LANES, preferred_element_type=F32
            )
        return carry

    gc[...] = jnp.zeros(gc.shape, F32)
    adjoint = turned[pl.ds(0, COUT, stride=16), :].astype(BF16)
    for a in range(3):
        gc[a, 0:PAD, :] = lax.dot_general(
            first_column(east_ref, west_ref, a), adjoint, OVER_LANES, preferred_element_type=F32
        )
    z_copy.wait()
    lax.fori_loop(0, 8, conv_grads, 0, unroll=4)
    left[...] = jnp.zeros(left.shape, F32)
    for tap in range(9):
        a, b = divmod(tap, 3)
        for half in range(2):
            lanes = slice(half * 128, (half + 1) * 128)
            for g in range(8):
                out_ref[96 + (tap * 8 + g) * 2 + half] = (
                    gc[a, b * PAD + g * 8:b * PAD + g * 8 + 8, lanes].astype(BF16)
                )
            at = 5 * (2 * tap + half)
            left[at:at + 5, :] = gc[a, b * PAD + 64:b * PAD + CIN, lanes]
    for m in range(16):
        out_ref[240 + m] = left[m * 8:(m + 1) * 8, :].astype(BF16)


def run_adjoint(coords, core, own, other, z, east, west, codes, cot):
    return vmem_call(
        adjoint_kernel,
        (
            jax.ShapeDtypeStruct((NBLK, TOK, 128), BF16),
            jax.ShapeDtypeStruct((256, 8, 128), BF16),
        ),
        [
            pltpu.VMEM((NBLK, TOK, 128), BF16),
            pltpu.VMEM((NBLK, TOK, 128), F32),
            pltpu.VMEM((WIDTH, TOK), F32),
            pltpu.VMEM((3, 3 * PAD, COUT), F32),
            pltpu.VMEM((128, 128), F32),
            pltpu.VMEM((3, 33 * PAD, 128), BF16),
            pltpu.SemaphoreType.DMA,
        ],
        1500 * 10**6, 8 * 10**6,
        coords, core, own, other, z, east, west, codes, cot, smem=2, hbm=(4,),
    )


def forward_kernel(
    coords_ref, core_ref, own_ref, other_ref, latent_ref, east_ref, west_ref, weight_ref,
    table_ref, codes_ref, adjoint_ref, cot_ref,
    state_ref, keep_ref, send_ref,
    sums, states, adjoints, wf,
):
    low_first = core_ref[0] == 0
    extra = jnp.zeros((COUT, TOK), F32)
    wf[...] = jnp.zeros(wf.shape, F32)
    for a in range(3):
        wf[0:CIN, :] = weight_ref[3 * a].astype(F32)
        extra += lax.dot_general(
            wf[...].astype(BF16), first_column(east_ref, west_ref, a), OVER_ROWS,
            preferred_element_type=F32,
        )
    at = pl.ds(0, COUT, stride=16)
    sums[...] = latent_ref[...]
    sums[at, :] = sums[at, :] + extra
    hot = hot_codes(codes_ref, 0)
    for b in range(NBLK):
        rows = slice(b * 128, (b + 1) * 128)
        state = sums[rows, :].astype(BF16)
        states[rows, 0:128] = state
        forcing = lax.dot_general(table_ref[:, rows], hot, OVER_ROWS, preferred_element_type=F32)
        sums[rows, :] = state.astype(F32) + forcing
        adjoints[b, 0:128, :] = adjoint_ref[b]
        adjoints[b, 128:256, :] = cot_ref[:, rows]
    push(
        coords_ref, low_first, own_ref, other_ref,
        lambda i: states[rows_of(i), 0:128], sums,
    )

    def end(b, carry):
        rows = rows_of(b)
        state = sums[rows, :].astype(BF16)
        states[rows, 128:256] = state
        state_ref[rows, :] = state
        return carry

    lax.fori_loop(0, NBLK, end, 0, unroll=4)

    def block_grads(group, carry):
        for u in range(UNROLL):
            n = group * UNROLL + u
            i, j = coords_ref[n, 0], coords_ref[n, 1]
            grad = dot(states[rows_of(i), :], adjoints[j])
            low, high = grad[0:64], grad[64:128]
            keep = jnp.where(low_first, low, high)
            send = jnp.where(low_first, high, low).astype(BF16)
            for x in range(2):
                keep_ref[x, n] = keep[x * 32:(x + 1) * 32]
                send_ref[x, n] = send[x * 32:(x + 1) * 32]
        return carry

    lax.fori_loop(0, NNZ // UNROLL, block_grads, 0)


def run_forward(coords, core, own, other, latent, east, west, weight, table, codes, adjoint, cot):
    return vmem_call(
        forward_kernel,
        (
            jax.ShapeDtypeStruct((WIDTH, TOK), BF16),
            jax.ShapeDtypeStruct((2, NNZ, 32, 128), F32),
            jax.ShapeDtypeStruct((2, NNZ, 32, 128), BF16),
        ),
        [
            pltpu.VMEM((WIDTH, TOK), F32),
            pltpu.VMEM((WIDTH, 2 * TOK), BF16),
            pltpu.VMEM((NBLK, 2 * TOK, 128), BF16),
            pltpu.VMEM((PAD, COUT), F32),
        ],
        1000, 1000,
        coords, core, own, other, latent, east, west, weight, table, codes, adjoint, cot, smem=2,
    )


def last_kernel(
    coords_ref, core_ref, own_ref, other_ref, state_ref, table_ref, codes_ref, next_ref, sums,
):
    low_first = core_ref[0] == 0
    hot = hot_codes(codes_ref, 1)
    for b in range(NBLK):
        rows = slice(b * 128, (b + 1) * 128)
        forcing = lax.dot_general(table_ref[:, rows], hot, OVER_ROWS, preferred_element_type=F32)
        sums[rows, :] = state_ref[rows, :].astype(F32) + forcing
    push(coords_ref, low_first, own_ref, other_ref, lambda i: state_ref[rows_of(i), :], sums)
    for b in range(NBLK):
        rows = slice(b * 128, (b + 1) * 128)
        next_ref[:, rows] = sums[rows, :].T.astype(BF16)


def run_last(coords, core, own, other, state, table, codes):
    return vmem_call(
        last_kernel,
        (jax.ShapeDtypeStruct((TOK, WIDTH), BF16),),
        [pltpu.VMEM((WIDTH, TOK), F32)],
        1000, 1000,
        coords, core, own, other, state, table, codes, smem=2,
    )[0]


def unpack_kernel(core_ref, own_ref, other_ref, conv_ref, forcing_ref, left):
    low_first = core_ref[0] == 0
    tiles = {}
    for p in range(16):
        for pair in range(4):
            own = own_ref[p, pair * 16:pair * 16 + 16, :].astype(F32)
            other = other_ref[p, pair * 16:pair * 16 + 16, :].astype(F32)
            both = (jnp.where(low_first, own, other), jnp.where(low_first, other, own))
            xl, yx = divmod(p, 8)
            for core in range(2):
                for z in range(2):
                    m = xl * 128 + core * 64 + yx * 8 + pair * 2 + z
                    tiles[m] = both[core][z * 8:z * 8 + 8]
    for j in range(NBLK):
        for third in range(3):
            forcing_ref[third * 8:(third + 1) * 8, j * 128:(j + 1) * 128] = tiles[3 * j + third]
    for m in range(12):
        left[m * 8:(m + 1) * 8, :] = tiles[240 + m]
    for tap in range(9):
        for half in range(2):
            lanes = slice(half * 128, (half + 1) * 128)
            for g in range(8):
                conv_ref[tap, g * 8:(g + 1) * 8, lanes] = tiles[96 + (tap * 8 + g) * 2 + half]
            at = 5 * (2 * tap + half)
            conv_ref[tap, 64:CIN, lanes] = left[at:at + 5, :]


def unpack(core, own, other):
    return vmem_call(
        unpack_kernel,
        (
            jax.ShapeDtypeStruct((9, CIN, COUT), F32),
            jax.ShapeDtypeStruct((NCODE, WIDTH), F32),
        ),
        [pltpu.VMEM((96, 128), F32)],
        1000, 1000, core, own, other, smem=1,
    )


def per_device(
    fields, conv_weight, kernel_blocks, block_coords, forcing_table, forcing_codes, cotangent
):
    core = lax.axis_index("core")
    top = jnp.pad(fields[:, :, 7, :], ((0, 0), (0, PAD - CIN), (0, 0))).reshape(4 * PAD, 256)

    which = core.astype(jnp.int32).reshape(1)
    copies = prepare(block_coords, which, kernel_blocks)
    copies, top = lax.optimization_barrier((copies, top))
    north = lax.ppermute(top, BAND, [(i, i + 1) for i in range(63)])
    column = lax.all_to_all(copies, "z", 0, 0, tiled=True)
    column, north = lax.optimization_barrier((column, north))
    own = lax.all_to_all(
        jnp.broadcast_to(column[None], (8,) + column.shape), ("y", "xh"), 0, 0, tiled=True
    ).reshape(NNZ, 72, 128)
    z, east = make_patches(fields.reshape(-1, 256), north)
    west = lax.ppermute(east, SECTION, [(i, (i + 1) % 4) for i in range(4)])
    latent = encode(z, conv_weight)
    own, latent = lax.optimization_barrier((own, latent))
    other = lax.ppermute(own, "core", [(0, 1), (1, 0)])
    coords = own[:, 64, 0:2].astype(jnp.int32)
    codes = forcing_codes.reshape(2, TOK)
    cot = cotangent.reshape(TOK, WIDTH)

    adjoint, partial = run_adjoint(coords, which, own, other, z, east, west, codes, cot)
    terms = lax.all_to_all(
        partial.reshape(32, 64, 128), ("xl", "core", "y", "xh"), 0, 0, tiled=True
    )
    state, keep, send = run_forward(
        coords, which, own, other, latent, east, west, conv_weight, forcing_table, codes,
        adjoint, cot,
    )
    terms, send = lax.optimization_barrier((terms, send))
    received = lax.ppermute(send, "core", [(0, 1), (1, 0)])
    latent_next = run_last(coords, which, own, other, state, forcing_table, codes)
    shared = jnp.sum(terms.astype(F32), axis=0).astype(BF16)
    spread = lax.all_to_all(
        jnp.broadcast_to(shared[None], (8, 64, 128)), "z", 0, 0, tiled=True
    )
    chip = (keep + received.astype(F32)).astype(BF16).reshape(16, 256, 128)
    spread, chip = lax.optimization_barrier((spread, chip))
    column = jnp.sum(spread.astype(F32), axis=0).astype(BF16)
    plane = lax.all_to_all(
        jnp.concatenate([chip, jnp.broadcast_to(column[None], (16, 64, 128))], axis=1),
        ("xl", "y", "xh"), 0, 0, tiled=True,
    )
    plane, latent_next = lax.optimization_barrier((plane, latent_next))
    half_sums = plane[:, 256:320]
    other_sums = lax.ppermute(half_sums, "core", [(0, 1), (1, 0)])
    grad_conv, grad_forcing = unpack(which, half_sums, other_sums)
    quarter = jnp.sum(plane[:, 0:256].astype(F32), axis=0).astype(BF16).reshape(8, 32, 128)
    parts = lax.all_to_all(
        jnp.broadcast_to(quarter[None], (4, 8, 32, 128)).reshape(32, 32, 128),
        ("xl", "core", "z"), 0, 0, tiled=True,
    )
    quarters = jnp.sum(parts.reshape(2, 2, 8, 32, 128).astype(F32), axis=2)
    grad_blocks = jnp.transpose(quarters, (1, 0, 2, 3)).reshape(1, 128, 128)
    return (latent_next.reshape(cotangent.shape), grad_conv, grad_blocks, grad_forcing)


def solution(mesh):
    fine = Mesh(mesh.devices.reshape(2, 2, 4, 2, 8), ALL)
    return jax.shard_map(
        per_device,
        mesh=fine,
        in_specs=(
            P(None, None, BAND, SECTION),
            P(),
            P(BAND, None, None),
            P(BAND, None),
            P(),
            P(None, None, BAND, SECTION),
            P(None, BAND, SECTION, None),
        ),
        out_specs=(P(None, BAND, SECTION, None), P(), P(BAND, None, None), P()),
        check_vma=False,
    )
```
